32 devices in a mesh: clip: 4 (over y, x), seq: 8 (over z, core).
Axes of the slice: x: 2, y: 2, z: 4, core: 2. Of those that a mesh axis runs over, the one named last changes fastest.
Arguments:
- tokens: bfloat16 [81920, 1280], P(('clip', 'seq')), parts along dimension 0, may hold values from -6 to 6
- slot_proj: bfloat16 [1280, 16], replicated, may hold values from -5 to 5, as said below
- w_in: bfloat16 [8, 1280, 2560], P('seq'), may hold values from -0.15625 to 0.15625
- w_out: bfloat16 [8, 2560, 1280], P('seq'), may hold values from -0.125 to 0.125
Outputs:
- mixed: bfloat16 [81920, 1280], P(('clip', 'seq')), parts along dimension 0
The draws below stay inside these ranges and needn't reach their ends.
There are 4 independent parts, one for each index of `clip`. The reference program is written for one: setup_inputs(seed, part) draws one part's arguments, and reference() takes and returns one part's arrays. A program takes and returns all parts, laid end to end along the dimension named above; an argument that names none is the same for every part. Nothing has to cross between parts.
Inputs may be any that keep to these rules, and one draw needn't show every extreme that they name: `slot_proj`: the slots' parameters.
All inputs are finite; a program needn't handle non-finite values.
Results may differ from the reference program's by a relative error of at most 0.02.
Values may be sent and summed in bfloat16 or wider, within the bound.
A program may use at most 64 MiB of HBM per device.

```python
import jax
import jax.numpy as jnp
from jax import lax

D = 1280
FF = 2560
SLOTS = 2
TOKENS = 20480
EXPERTS = 8
SLOTS_ALL = 16


def draw_slot_proj(key, part):
    key = jax.random.fold_in(key, 11)
    base_key, scale_key = jax.random.split(key)
    values = jax.random.truncated_normal(base_key, -4.0, 4.0, (D, SLOTS_ALL), jnp.float32)
    column_scale = jnp.exp(jax.random.uniform(scale_key, (1, SLOTS_ALL), jnp.float32, jnp.log(4.0), jnp.log(16.0)))
    scaled = jnp.clip(values * column_scale / jnp.sqrt(jnp.float32(D)), -5.0, 5.0)
    return scaled.astype(jnp.bfloat16)


def shard_levels(rng, extent, cuts, smallest, top_value):
    factor_of = 1.0
    for axis_at, shards_of in cuts:
        steps = jax.random.uniform(jax.random.fold_in(jax.random.fold_in(rng, 6), axis_at), (shards_of,), jnp.float32, smallest / len(cuts), top_value / len(cuts))
        factor_of = factor_of * jnp.repeat(jnp.exp(steps), extent[axis_at] // shards_of).reshape((-1,) + (1,) * (len(extent) - 1 - axis_at))
    return factor_of


def normal_values(stream_key, shape, spread, most, shards=(), dtype=jnp.bfloat16):
    entries = spread * jax.random.normal(stream_key, shape, jnp.float32)
    if shards:
        entries = entries * shard_levels(stream_key, shape, shards, -0.22, 0.18)
    return jnp.clip(entries, -most, most).astype(dtype)


def setup_inputs(seed: int = 0, part: int = 0) -> dict:
    key_of = jax.random.split(jax.random.key(seed), 5)
    part_keys = jax.random.split(jax.random.fold_in(key_of[4], part), 5)
    return {
        "tokens": normal_values(part_keys[0], (TOKENS, D), 1.0, 6.0, ((0, 8),)),
        "slot_proj": draw_slot_proj(jax.random.fold_in(key_of[4], 71), part),
        "w_in": normal_values(key_of[2], (EXPERTS, D, FF), D ** -0.5, 0.15625, ((0, 8),)),
        "w_out": normal_values(key_of[3], (EXPERTS, FF, D), FF ** -0.5, 0.125, ((0, 8),)),
    }


def run_expert(packed):
    slot_in, first, second = packed
    hidden = jax.nn.gelu(jnp.dot(slot_in, first, preferred_element_type=jnp.float32)).astype(jnp.bfloat16)
    return jnp.dot(hidden, second, preferred_element_type=jnp.float32).astype(jnp.bfloat16)


def reference(tokens, slot_proj, w_in, w_out):
    logits = jnp.dot(tokens, slot_proj, preferred_element_type=jnp.float32)
    col_max = jnp.max(logits, axis=0)
    shifted = jnp.exp(logits - col_max[None, :])
    col_total = jnp.sum(shifted, axis=0)
    dispatch = shifted.astype(jnp.bfloat16)
    slot_num = jnp.dot(dispatch.T, tokens, preferred_element_type=jnp.float32)
    slot_in = (slot_num / col_total[:, None]).astype(jnp.bfloat16)
    slot_in = slot_in.reshape(EXPERTS, SLOTS, D)
    slot_out = lax.map(run_expert, (slot_in, w_in, w_out)).reshape(SLOTS_ALL, D)
    combine = jax.nn.softmax(logits, axis=1).astype(jnp.bfloat16)
    return jnp.dot(combine, slot_out, preferred_element_type=jnp.float32).astype(jnp.bfloat16)
```

```python
import functools

import jax
import jax.numpy as jnp
from jax import lax
from jax.experimental import pallas as pl
from jax.experimental.pallas import tpu as pltpu
from jax.sharding import PartitionSpec as P

MESH = pl.DeviceIdType.MESH
F32 = jnp.float32
BF16 = jnp.bfloat16
TOKEN_PARTS = 5
FF_PARTS = 4
STAT = 128


def route_kernel(
    n,
    tokens_hbm,
    proj_hbm,
    w_in_hbm,
    w_out_hbm,
    combine_ref,
    slots_ref,
    tok,
    proj,
    w_in,
    w_out,
    logits,
    send,
    recv,
    gather,
    rows,
    tok_sem,
    proj_sem,
    in_sem,
    out_sem,
    s1_sem,
    r1_sem,
    s2_sem,
    r2_sem,
):
    me = lax.axis_index("seq")
    width = tok.shape[1]
    slots = send.shape[1]
    part = tok.shape[0] // TOKEN_PARTS
    ff = w_in.shape[1]
    ff_part = ff // FF_PARTS

    proj_copy = pltpu.make_async_copy(proj_hbm, proj, proj_sem)
    proj_copy.start()
    tok_copies = []
    for c in range(TOKEN_PARTS):
        at = pl.ds(c * part, part)
        copy = pltpu.make_async_copy(tokens_hbm.at[at, :], tok.at[at, :], tok_sem.at[c])
        copy.start()
        tok_copies.append(copy)
    in_copies, out_copies = [], []
    for c in range(FF_PARTS):
        at = pl.ds(c * ff_part, ff_part)
        copy = pltpu.make_async_copy(w_in_hbm.at[0, :, at], w_in.at[:, at], in_sem.at[c])
        copy.start()
        in_copies.append(copy)
        copy = pltpu.make_async_copy(w_out_hbm.at[0, at, :], w_out.at[at, :], out_sem.at[c])
        copy.start()
        out_copies.append(copy)

    barrier = pltpu.get_barrier_semaphore()
    peers = [lax.rem(me + off, n) for off in range(1, n)]
    for peer in peers:
        pl.semaphore_signal(barrier, inc=1, device_id={"seq": peer}, device_id_type=MESH)

    proj_copy.wait()
    proj_cols = proj[...].T
    top = total = num = None
    for c in range(TOKEN_PARTS):
        tok_copies[c].wait()
        x = tok[c * part : (c + 1) * part, :]
        l = jnp.dot(x, proj_cols, preferred_element_type=F32).T
        logits[:, c * part : (c + 1) * part] = l
        here = jnp.max(l, axis=1, keepdims=True)
        new = here if c == 0 else jnp.maximum(top, here)
        shifted = jnp.exp(l - new)
        t = jnp.sum(shifted, axis=1, keepdims=True)
        v = jnp.dot(shifted.astype(BF16), x, preferred_element_type=F32)
        if c == 0:
            total, num = t, v
        else:
            keep = jnp.exp(top - new)
            total, num = total * keep + t, num * keep + v
        top = new

    for e in range(n):
        at = slice(e * slots, (e + 1) * slots)
        send[e, :, :width] = num[at, :]
        send[e, :, width : width + STAT] = jnp.broadcast_to(top[at, :], (slots, STAT))
        send[e, :, width + STAT :] = jnp.broadcast_to(total[at, :], (slots, STAT))

    pl.semaphore_wait(barrier, n - 1)
    first = []
    for k, peer in enumerate(peers):
        copy = pltpu.make_async_remote_copy(
            src_ref=send.at[peer],
            dst_ref=recv.at[k],
            send_sem=s1_sem.at[k],
            recv_sem=r1_sem.at[k],
            device_id={"seq": peer},
            device_id_type=MESH,
        )
        copy.start()
        first.append(copy)

    l = logits[...]
    e = jnp.exp(l - jnp.max(l, axis=0, keepdims=True))
    combine_ref[...] = (e / jnp.sum(e, axis=0, keepdims=True)).astype(BF16)

    for copy in first:
        copy.wait_recv()
    own = send[me]
    tops = [own[:, width : width + STAT]] + [recv[k, :, width : width + STAT] for k in range(n - 1)]
    top = functools.reduce(jnp.maximum, tops)
    total = jnp.zeros((slots, STAT), F32)
    num = jnp.zeros((slots, width), F32)
    for k in range(n):
        scale = jnp.exp(tops[k] - top)
        got = own if k == 0 else recv[k - 1]
        total = total + scale * got[:, width + STAT :]
        num = num + scale[:, :1] * got[:, :width]
    slot_in = (num / total[:, :1]).astype(BF16)

    slot_out = jnp.zeros((slots, width), F32)
    for c in range(FF_PARTS):
        at = slice(c * ff_part, (c + 1) * ff_part)
        in_copies[c].wait()
        hidden = jnp.dot(slot_in, w_in[:, at], preferred_element_type=F32)
        hidden = jax.nn.gelu(hidden).astype(BF16)
        out_copies[c].wait()
        slot_out = slot_out + jnp.dot(hidden, w_out[at, :], preferred_element_type=F32)
    gather[me] = slot_out.astype(BF16).astype(F32)

    second = []
    for k, peer in enumerate(peers):
        copy = pltpu.make_async_remote_copy(
            src_ref=gather.at[me],
            dst_ref=gather.at[me],
            send_sem=s2_sem.at[k],
            recv_sem=r2_sem.at[k],
            device_id={"seq": peer},
            device_id_type=MESH,
        )
        copy.start()
        second.append(copy)
    for copy in second:
        copy.wait_recv()
    for e in range(n):
        rows[e * slots : (e + 1) * slots, :] = gather[e]
    slots_ref[...] = rows[...].astype(BF16)
    for copy in first + second:
        copy.wait_send()


def mix_kernel(combine_ref, slots_ref, out_ref):
    out_ref[...] = lax.dot_general(
        combine_ref[...], slots_ref[...], (((0,), (0,)), ((), ())), preferred_element_type=F32
    ).astype(BF16)


def body(n, tokens, slot_proj, w_in, w_out):
    count, width = tokens.shape
    slots_all = slot_proj.shape[1]
    slots = slots_all // n
    ff = w_in.shape[2]
    assert w_in.shape[0] == 1
    any_spec = pl.BlockSpec(memory_space=pl.ANY)
    vmem_spec = pl.BlockSpec(memory_space=pltpu.VMEM)
    wide = width + 2 * STAT
    dma = pltpu.SemaphoreType.DMA
    combine, slot_out = pl.pallas_call(
        functools.partial(route_kernel, n),
        out_shape=[
            jax.ShapeDtypeStruct((slots_all, count), BF16),
            jax.ShapeDtypeStruct((slots_all, width), BF16),
        ],
        in_specs=[any_spec] * 4,
        out_specs=[vmem_spec] * 2,
        scratch_shapes=[
            pltpu.VMEM((count, width), BF16),
            pltpu.VMEM((slots_all, width), BF16),
            pltpu.VMEM((width, ff), BF16),
            pltpu.VMEM((ff, width), BF16),
            pltpu.VMEM((slots_all, count), F32),
            pltpu.VMEM((n, slots, wide), F32),
            pltpu.VMEM((n - 1, slots, wide), F32),
            pltpu.VMEM((n, slots, width), F32),
            pltpu.VMEM((slots_all, width), F32),
            dma((TOKEN_PARTS,)),
            dma,
            dma((FF_PARTS,)),
            dma((FF_PARTS,)),
            dma((n - 1,)),
            dma((n - 1,)),
            dma((n - 1,)),
            dma((n - 1,)),
        ],
        compiler_params=pltpu.CompilerParams(
            collective_id=0, has_side_effects=True, vmem_limit_bytes=48 * 1024 * 1024
        ),
        cost_estimate=pl.CostEstimate(
            flops=4 * count * width * slots_all + 4 * slots * width * ff,
            bytes_accessed=2 * (count * width + 2 * width * ff),
            transcendentals=2 * count * slots_all,
        ),
        name="route",
    )(tokens, slot_proj.T, w_in, w_out)
    part = count // TOKEN_PARTS
    return pl.pallas_call(
        mix_kernel,
        grid=(TOKEN_PARTS,),
        out_shape=jax.ShapeDtypeStruct((count, width), BF16),
        in_specs=[
            pl.BlockSpec((slots_all, part), lambda i: (0, i)),
            pl.BlockSpec((slots_all, width), lambda i: (0, 0)),
        ],
        out_specs=pl.BlockSpec((part, width), lambda i: (i, 0)),
        compiler_params=pltpu.CompilerParams(vmem_limit_bytes=32 * 1024 * 1024),
        cost_estimate=pl.CostEstimate(
            flops=2 * count * width * slots_all,
            bytes_accessed=2 * count * width,
            transcendentals=0,
        ),
        name="mix",
    )(combine, slot_out)


def solution(mesh):
    return jax.shard_map(
        functools.partial(body, mesh.shape["seq"]),
        mesh=mesh,
        in_specs=(P(("clip", "seq"), None), P(), P("seq", None, None), P("seq", None, None)),
        out_specs=P(("clip", "seq"), None),
        check_vma=False,
    )
```

```python
import functools

import jax
import jax.numpy as jnp
from jax import lax
from jax.experimental import pallas as pl
from jax.experimental.pallas import tpu as pltpu
from jax.sharding import PartitionSpec as P

MESH = pl.DeviceIdType.MESH
F32 = jnp.float32
BF16 = jnp.bfloat16
TOKEN_PARTS = 5
FF_PARTS = 4
MIX_PARTS = 10
STAT = 128


def route_kernel(
    n,
    tokens_hbm,
    proj_hbm,
    w_in_hbm,
    w_out_hbm,
    combine_ref,
    slots_ref,
    tok,
    proj,
    w_in,
    w_out,
    logits,
    send,
    recv,
    gather,
    rows,
    tok_sem,
    proj_sem,
    in_sem,
    out_sem,
    s1_sem,
    r1_sem,
    s2_sem,
    r2_sem,
):
    me = lax.axis_index("seq")
    width = tok.shape[1]
    slots = send.shape[1]
    part = tok.shape[0] // TOKEN_PARTS
    ff = w_in.shape[1]
    ff_part = ff // FF_PARTS

    proj_copy = pltpu.make_async_copy(proj_hbm, proj, proj_sem)
    proj_copy.start()
    tok_copies = []
    for c in range(TOKEN_PARTS):
        at = pl.ds(c * part, part)
        copy = pltpu.make_async_copy(tokens_hbm.at[at, :], tok.at[at, :], tok_sem.at[c])
        copy.start()
        tok_copies.append(copy)
    in_copies, out_copies = [], []
    for c in range(FF_PARTS):
        at = pl.ds(c * ff_part, ff_part)
        in_copies.append(pltpu.make_async_copy(w_in_hbm.at[0, :, at], w_in.at[:, at], in_sem.at[c]))
        out_copies.append(pltpu.make_async_copy(w_out_hbm.at[0, at, :], w_out.at[at, :], out_sem.at[c]))

    barrier = pltpu.get_barrier_semaphore()
    peers = [lax.rem(me + off, n) for off in range(1, n)]
    for peer in peers:
        pl.semaphore_signal(barrier, inc=1, device_id={"seq": peer}, device_id_type=MESH)

    proj_copy.wait()
    proj_cols = proj[...].T

    def part_logits(c):
        tok_copies[c].wait()
        at = slice(c * part, (c + 1) * part)
        l = jnp.dot(tok[at, :], proj_cols, preferred_element_type=F32).T
        logits[:, at] = l
        return l

    top = total = num = None
    l = part_logits(0)
    for c in range(TOKEN_PARTS):
        if c + 1 < TOKEN_PARTS:
            following = part_logits(c + 1)
            if c + 2 == TOKEN_PARTS:
                for copy in in_copies + out_copies:
                    copy.start()
        here = jnp.max(l, axis=1, keepdims=True)
        new = here if c == 0 else jnp.maximum(top, here)
        shifted = jnp.exp(l - new)
        t = jnp.sum(shifted, axis=1, keepdims=True)
        x = tok[c * part : (c + 1) * part, :]
        v = jnp.dot(shifted.astype(BF16), x, preferred_element_type=F32)
        if c == 0:
            total, num = t, v
        else:
            keep = jnp.exp(top - new)
            total, num = total * keep + t, num * keep + v
        top, l = new, following

    for e in range(n):
        at = slice(e * slots, (e + 1) * slots)
        send[e, :, :width] = num[at, :]
        send[e, :, width : width + STAT] = jnp.broadcast_to(top[at, :], (slots, STAT))
        send[e, :, width + STAT :] = jnp.broadcast_to(total[at, :], (slots, STAT))

    pl.semaphore_wait(barrier, n - 1)
    first = []
    for k, peer in enumerate(peers):
        copy = pltpu.make_async_remote_copy(
            src_ref=send.at[peer],
            dst_ref=recv.at[k],
            send_sem=s1_sem.at[k],
            recv_sem=r1_sem.at[k],
            device_id={"seq": peer},
            device_id_type=MESH,
        )
        copy.start()
        first.append(copy)

    l = logits[...]
    e = jnp.exp(l - jnp.max(l, axis=0, keepdims=True))
    combine_ref[...] = (e / jnp.sum(e, axis=0, keepdims=True)).T.astype(BF16)

    for copy in first:
        copy.wait_recv()
    own = send[me]
    tops = [own[:, width : width + STAT]] + [recv[k, :, width : width + STAT] for k in range(n - 1)]
    top = functools.reduce(jnp.maximum, tops)
    total = jnp.zeros((slots, STAT), F32)
    num = jnp.zeros((slots, width), F32)
    for k in range(n):
        scale = jnp.exp(tops[k] - top)
        got = own if k == 0 else recv[k - 1]
        total = total + scale * got[:, width + STAT :]
        num = num + scale[:, :1] * got[:, :width]
    slot_in = (num / total[:, :1]).astype(BF16)

    for copy in in_copies + out_copies:
        copy.wait()
    slot_out = jnp.zeros((slots, width), F32)
    for c in range(FF_PARTS):
        at = slice(c * ff_part, (c + 1) * ff_part)
        hidden = jnp.dot(slot_in, w_in[:, at], preferred_element_type=F32)
        hidden = jax.nn.gelu(hidden).astype(BF16)
        slot_out = slot_out + jnp.dot(hidden, w_out[at, :], preferred_element_type=F32)
    gather[me] = slot_out.astype(BF16).astype(F32)

    second = []
    for k, peer in enumerate(peers):
        copy = pltpu.make_async_remote_copy(
            src_ref=gather.at[me],
            dst_ref=gather.at[me],
            send_sem=s2_sem.at[k],
            recv_sem=r2_sem.at[k],
            device_id={"seq": peer},
            device_id_type=MESH,
        )
        copy.start()
        second.append(copy)
    for copy in second:
        copy.wait_recv()
    for e in range(n):
        rows[e * slots : (e + 1) * slots, :] = gather[e]
    slots_ref[...] = rows[...].astype(BF16)
    for copy in first + second:
        copy.wait_send()


def mix_kernel(combine_ref, slots_ref, out_hbm, out, out_sem):
    part = out.shape[0] // MIX_PARTS
    copies = []
    for c in range(MIX_PARTS):
        at = pl.ds(c * part, part)
        out[at, :] = jnp.dot(
            combine_ref[at, :], slots_ref[...], preferred_element_type=F32
        ).astype(BF16)
        copy = pltpu.make_async_copy(out.at[at, :], out_hbm.at[at, :], out_sem.at[c])
        copy.start()
        copies.append(copy)
    for copy in copies:
        copy.wait()


def body(n, tokens, slot_proj, w_in, w_out):
    count, width = tokens.shape
    slots_all = slot_proj.shape[1]
    slots = slots_all // n
    ff = w_in.shape[2]
    assert w_in.shape[0] == 1
    hbm_spec = pl.BlockSpec(memory_space=pltpu.HBM)
    vmem_spec = pl.BlockSpec(memory_space=pltpu.VMEM)
    wide = width + 2 * STAT
    dma = pltpu.SemaphoreType.DMA
    combine, slot_out = pl.pallas_call(
        functools.partial(route_kernel, n),
        out_shape=[
            jax.ShapeDtypeStruct((count, slots_all), BF16),
            jax.ShapeDtypeStruct((slots_all, width), BF16),
        ],
        in_specs=[hbm_spec] * 4,
        out_specs=[vmem_spec] * 2,
        scratch_shapes=[
            pltpu.VMEM((count, width), BF16),
            pltpu.VMEM((slots_all, width), BF16),
            pltpu.VMEM((width, ff), BF16),
            pltpu.VMEM((ff, width), BF16),
            pltpu.VMEM((slots_all, count), F32),
            pltpu.VMEM((n, slots, wide), F32),
            pltpu.VMEM((n - 1, slots, wide), F32),
            pltpu.VMEM((n, slots, width), F32),
            pltpu.VMEM((slots_all, width), F32),
            dma((TOKEN_PARTS,)),
            dma,
            dma((FF_PARTS,)),
            dma((FF_PARTS,)),
            dma((n - 1,)),
            dma((n - 1,)),
            dma((n - 1,)),
            dma((n - 1,)),
        ],
        compiler_params=pltpu.CompilerParams(
            collective_id=0, has_side_effects=True, vmem_limit_bytes=48 * 1024 * 1024
        ),
        cost_estimate=pl.CostEstimate(
            flops=4 * count * width * slots_all + 4 * slots * width * ff,
            bytes_accessed=2 * (count * width + 2 * width * ff),
            transcendentals=2 * count * slots_all,
        ),
        name="route",
    )(tokens, pltpu.with_memory_space_constraint(slot_proj.T, pltpu.HBM), w_in, w_out)
    return pl.pallas_call(
        mix_kernel,
        out_shape=jax.ShapeDtypeStruct((count, width), BF16),
        in_specs=[vmem_spec] * 2,
        out_specs=hbm_spec,
        scratch_shapes=[pltpu.VMEM((count, width), BF16), dma((MIX_PARTS,))],
        compiler_params=pltpu.CompilerParams(vmem_limit_bytes=32 * 1024 * 1024),
        cost_estimate=pl.CostEstimate(
            flops=2 * count * width * slots_all,
            bytes_accessed=2 * count * width,
            transcendentals=0,
        ),
        name="mix",
    )(combine, slot_out)


def solution(mesh):
    return jax.shard_map(
        functools.partial(body, mesh.shape["seq"]),
        mesh=mesh,
        in_specs=(P(("clip", "seq"), None), P(), P("seq", None, None), P("seq", None, None)),
        out_specs=P(("clip", "seq"), None),
        check_vma=False,
    )
```

```python
import functools

import jax
import jax.numpy as jnp
from jax import lax
from jax.experimental import pallas as pl
from jax.experimental.pallas import tpu as pltpu
from jax.sharding import PartitionSpec as P

MESH = pl.DeviceIdType.MESH
F32 = jnp.float32
BF16 = jnp.bfloat16
TOKEN_PARTS = 5
FF_PARTS = 5
MIX_PARTS = 10
STAT = 128


def split3(x):
    high = x.astype(BF16).astype(F32)
    middle = (x - high).astype(BF16).astype(F32)
    return [high, middle, x - high - middle]


def route_kernel(
    n,
    tokens_hbm,
    proj_hbm,
    w_in_hbm,
    w_out_hbm,
    combine_ref,
    slots_ref,
    tok,
    proj,
    w_in,
    w_out,
    logits,
    send,
    recv,
    gather,
    rows,
    tok_sem,
    proj_sem,
    in_sem,
    out_sem,
    s1_sem,
    r1_sem,
    s2_sem,
    r2_sem,
):
    me = lax.axis_index("seq")
    width = tok.shape[1]
    slots = send.shape[1]
    part = tok.shape[0] // TOKEN_PARTS
    ff = w_in.shape[1]
    ff_part = ff // FF_PARTS

    proj_copy = pltpu.make_async_copy(proj_hbm, proj, proj_sem)
    proj_copy.start()
    tok_copies = []
    for c in range(TOKEN_PARTS):
        at = pl.ds(c * part, part)
        copy = pltpu.make_async_copy(tokens_hbm.at[at, :], tok.at[at, :], tok_sem.at[c])
        copy.start()
        tok_copies.append(copy)
    in_copies, out_copies = [], []
    for c in range(FF_PARTS):
        at = pl.ds(c * ff_part, ff_part)
        in_copies.append(pltpu.make_async_copy(w_in_hbm.at[0, :, at], w_in.at[:, at], in_sem.at[c]))
        out_copies.append(pltpu.make_async_copy(w_out_hbm.at[0, at, :], w_out.at[at, :], out_sem.at[c]))

    barrier = pltpu.get_barrier_semaphore()
    peers = [lax.bitwise_xor(me, n - 1 - k) for k in range(n - 1)]
    for peer in peers:
        pl.semaphore_signal(barrier, inc=1, device_id={"seq": peer}, device_id_type=MESH)

    proj_copy.wait()
    proj_cols = proj[...].T

    def part_logits(c):
        tok_copies[c].wait()
        at = slice(c * part, (c + 1) * part)
        l = jnp.dot(tok[at, :], proj_cols, preferred_element_type=F32).T
        logits[:, at] = l
        return l

    top = total = num = None
    l = part_logits(0)
    for c in range(TOKEN_PARTS):
        if c + 1 < TOKEN_PARTS:
            following = part_logits(c + 1)
            if c + 2 == TOKEN_PARTS:
                for copy in in_copies + out_copies:
                    copy.start()
        here = jnp.max(l, axis=1, keepdims=True)
        new = here if c == 0 else jnp.maximum(top, here)
        shifted = jnp.exp(l - new)
        t = jnp.sum(shifted, axis=1, keepdims=True)
        x = tok[c * part : (c + 1) * part, :]
        v = jnp.dot(shifted.astype(BF16), x, preferred_element_type=F32)
        if c == 0:
            total, num = t, v
        else:
            keep = jnp.exp(top - new)
            total, num = total * keep + t, num * keep + v
        top, l = new, following

    lane = lax.broadcasted_iota(jnp.int32, (num.shape[0], STAT), 1)
    stats = jnp.zeros((num.shape[0], STAT), F32)
    for i, term in enumerate(split3(top) + split3(total)):
        stats = jnp.where(lane == i, term, stats)
    for e in range(n):
        at = slice(e * slots, (e + 1) * slots)
        send[e, :, :width] = num[at, :].astype(BF16)
        send[e, :, width:] = stats[at, :].astype(BF16)

    pl.semaphore_wait(barrier, n - 1)
    first = []
    for k, peer in enumerate(peers):
        copy = pltpu.make_async_remote_copy(
            src_ref=send.at[peer],
            dst_ref=recv.at[k],
            send_sem=s1_sem.at[k],
            recv_sem=r1_sem.at[k],
            device_id={"seq": peer},
            device_id_type=MESH,
        )
        copy.start()
        first.append(copy)

    l = logits[...]
    e = jnp.exp(l - jnp.max(l, axis=0, keepdims=True))
    combine_ref[...] = (e / jnp.sum(e, axis=0, keepdims=True)).T.astype(BF16)

    for copy in first:
        copy.wait_recv()
    got = [send[me].astype(F32)] + [recv[k].astype(F32) for k in range(n - 1)]
    terms = [[g[:, width + i : width + i + 1] for i in range(6)] for g in got]
    tops = [t[0] + t[1] + t[2] for t in terms]
    top = functools.reduce(jnp.maximum, tops)
    total = jnp.zeros((slots, 1), F32)
    num = jnp.zeros((slots, width), F32)
    for k in range(n):
        scale = jnp.exp(tops[k] - top)
        total = total + scale * (terms[k][3] + terms[k][4] + terms[k][5])
        num = num + scale * got[k][:, :width]
    slot_in = (num / total).astype(BF16)

    for copy in in_copies + out_copies:
        copy.wait()
    slot_out = jnp.zeros((slots, width), F32)
    for c in range(FF_PARTS):
        at = slice(c * ff_part, (c + 1) * ff_part)
        hidden = jnp.dot(slot_in, w_in[:, at], preferred_element_type=F32)
        hidden = jax.nn.gelu(hidden).astype(BF16)
        slot_out = slot_out + jnp.dot(hidden, w_out[at, :], preferred_element_type=F32)
    gather[me] = slot_out.astype(BF16)

    second = []
    for k, peer in enumerate(peers):
        copy = pltpu.make_async_remote_copy(
            src_ref=gather.at[me],
            dst_ref=gather.at[me],
            send_sem=s2_sem.at[k],
            recv_sem=r2_sem.at[k],
            device_id={"seq": peer},
            device_id_type=MESH,
        )
        copy.start()
        second.append(copy)
    for copy in second:
        copy.wait_recv()
    for e in range(n):
        rows[e * slots : (e + 1) * slots, :] = gather[e].astype(F32)
    slots_ref[...] = rows[...].astype(BF16)
    for copy in first + second:
        copy.wait_send()


def mix_kernel(combine_ref, slots_ref, out_hbm, out, out_sem):
    part = out.shape[0] // MIX_PARTS
    copies = []
    for c in range(MIX_PARTS):
        at = pl.ds(c * part, part)
        out[at, :] = jnp.dot(
            combine_ref[at, :], slots_ref[...], preferred_element_type=F32
        ).astype(BF16)
        copy = pltpu.make_async_copy(out.at[at, :], out_hbm.at[at, :], out_sem.at[c])
        copy.start()
        copies.append(copy)
    for copy in copies:
        copy.wait()


def body(n, tokens, slot_proj, w_in, w_out):
    count, width = tokens.shape
    slots_all = slot_proj.shape[1]
    slots = slots_all // n
    ff = w_in.shape[2]
    assert w_in.shape[0] == 1 and n & (n - 1) == 0
    hbm_spec = pl.BlockSpec(memory_space=pltpu.HBM)
    vmem_spec = pl.BlockSpec(memory_space=pltpu.VMEM)
    wide = width + STAT
    dma = pltpu.SemaphoreType.DMA
    combine, slot_out = pl.pallas_call(
        functools.partial(route_kernel, n),
        out_shape=[
            jax.ShapeDtypeStruct((count, slots_all), BF16),
            jax.ShapeDtypeStruct((slots_all, width), BF16),
        ],
        in_specs=[hbm_spec] * 4,
        out_specs=[vmem_spec] * 2,
        scratch_shapes=[
            pltpu.VMEM((count, width), BF16),
            pltpu.VMEM((slots_all, width), BF16),
            pltpu.VMEM((width, ff), BF16),
            pltpu.VMEM((ff, width), BF16),
            pltpu.VMEM((slots_all, count), F32),
            pltpu.VMEM((n, slots, wide), BF16),
            pltpu.VMEM((n - 1, slots, wide), BF16),
            pltpu.VMEM((n, slots, width), BF16),
            pltpu.VMEM((slots_all, width), F32),
            dma((TOKEN_PARTS,)),
            dma,
            dma((FF_PARTS,)),
            dma((FF_PARTS,)),
            dma((n - 1,)),
            dma((n - 1,)),
            dma((n - 1,)),
            dma((n - 1,)),
        ],
        compiler_params=pltpu.CompilerParams(
            collective_id=0, has_side_effects=True, vmem_limit_bytes=48 * 1024 * 1024
        ),
        cost_estimate=pl.CostEstimate(
            flops=4 * count * width * slots_all + 4 * slots * width * ff,
            bytes_accessed=2 * (count * width + 2 * width * ff),
            transcendentals=2 * count * slots_all,
        ),
        name="route",
    )(tokens, pltpu.with_memory_space_constraint(slot_proj.T, pltpu.HBM), w_in, w_out)
    return pl.pallas_call(
        mix_kernel,
        out_shape=jax.ShapeDtypeStruct((count, width), BF16),
        in_specs=[vmem_spec] * 2,
        out_specs=hbm_spec,
        scratch_shapes=[pltpu.VMEM((count, width), BF16), dma((MIX_PARTS,))],
        compiler_params=pltpu.CompilerParams(vmem_limit_bytes=32 * 1024 * 1024),
        cost_estimate=pl.CostEstimate(
            flops=2 * count * width * slots_all,
            bytes_accessed=2 * count * width,
            transcendentals=0,
        ),
        name="mix",
    )(combine, slot_out)


def solution(mesh):
    return jax.shard_map(
        functools.partial(body, mesh.shape["seq"]),
        mesh=mesh,
        in_specs=(P(("clip", "seq"), None), P(), P("seq", None, None), P("seq", None, None)),
        out_specs=P(("clip", "seq"), None),
        check_vma=False,
    )
```

```python
import functools

import jax
import jax.numpy as jnp
from jax import lax
from jax.experimental import pallas as pl
from jax.experimental.pallas import tpu as pltpu
from jax.sharding import PartitionSpec as P

MESH = pl.DeviceIdType.MESH
F32 = jnp.float32
BF16 = jnp.bfloat16
TOKEN_PARTS = 5
FF_PARTS = 5
MIX_PARTS = 10
GROUP = 256
STAT = 128


def split3(x):
    high = x.astype(BF16).astype(F32)
    middle = (x - high).astype(BF16).astype(F32)
    return [high, middle, x - high - middle]


def spread_slots(spread, x):
    slots, depth = x.shape
    columns = jnp.concatenate([x] * (8 // slots), axis=0).T
    for i in range(slots):
        spread[i, :depth, :] = jnp.broadcast_to(columns[:, i : i + 1], (depth, 128)).astype(BF16)


def vector_dot(spread, w, row, depth, column):
    slots = spread.shape[0]
    sums = [jnp.zeros((16, GROUP), F32) for _ in range(slots)]
    for d in range(0, depth, 64):
        tiles = [w[row + d + r : row + d + r + 16, column : column + GROUP] for r in range(0, 64, 16)]
        for i in range(slots):
            terms = []
            for k, tile in enumerate(tiles):
                value = spread[i, d + 16 * k : d + 16 * k + 16, :]
                terms.append(tile * jnp.concatenate([value] * (GROUP // 128), axis=1))
            pair = (terms[0] + terms[1]) + (terms[2] + terms[3])
            sums[i] = sums[i] + pair.astype(F32)
    return jnp.concatenate([jnp.sum(x, axis=0, keepdims=True) for x in sums], axis=0)


def route_kernel(
    n,
    tokens_hbm,
    proj_hbm,
    w_in_hbm,
    w_out_hbm,
    combine_ref,
    slots_ref,
    tok,
    proj,
    w_in,
    w_out,
    logits,
    send,
    recv,
    gather,
    rows,
    spread,
    tok_sem,
    proj_sem,
    in_sem,
    out_sem,
    s1_sem,
    r1_sem,
    s2_sem,
    r2_sem,
):
    me = lax.axis_index("seq")
    width = tok.shape[1]
    slots = send.shape[1]
    part = tok.shape[0] // TOKEN_PARTS
    ff = w_in.shape[1]
    ff_part = ff // FF_PARTS

    proj_copy = pltpu.make_async_copy(proj_hbm, proj, proj_sem)
    proj_copy.start()
    tok_copies = []
    for c in range(TOKEN_PARTS):
        at = pl.ds(c * part, part)
        copy = pltpu.make_async_copy(tokens_hbm.at[at, :], tok.at[at, :], tok_sem.at[c])
        copy.start()
        tok_copies.append(copy)
    in_copies, out_copies = [], []
    for c in range(FF_PARTS):
        at = pl.ds(c * ff_part, ff_part)
        in_copies.append(pltpu.make_async_copy(w_in_hbm.at[0, :, at], w_in.at[:, at], in_sem.at[c]))
        out_copies.append(pltpu.make_async_copy(w_out_hbm.at[0, at, :], w_out.at[at, :], out_sem.at[c]))

    barrier = pltpu.get_barrier_semaphore()
    peers = [lax.bitwise_xor(me, n - 1 - k) for k in range(n - 1)]
    for peer in peers:
        pl.semaphore_signal(barrier, inc=1, device_id={"seq": peer}, device_id_type=MESH)

    proj_copy.wait()
    proj_cols = proj[...].T

    def part_logits(c):
        tok_copies[c].wait()
        at = slice(c * part, (c + 1) * part)
        l = jnp.dot(tok[at, :], proj_cols, preferred_element_type=F32).T
        logits[:, at] = l
        return l

    top = total = num = None
    l = part_logits(0)
    for c in range(TOKEN_PARTS):
        if c + 1 < TOKEN_PARTS:
            following = part_logits(c + 1)
            if c + 2 == TOKEN_PARTS:
                for copy in in_copies + out_copies:
                    copy.start()
        here = jnp.max(l, axis=1, keepdims=True)
        new = here if c == 0 else jnp.maximum(top, here)
        shifted = jnp.exp(l - new)
        t = jnp.sum(shifted, axis=1, keepdims=True)
        x = tok[c * part : (c + 1) * part, :]
        v = jnp.dot(shifted.astype(BF16), x, preferred_element_type=F32)
        if c == 0:
            total, num = t, v
        else:
            keep = jnp.exp(top - new)
            total, num = total * keep + t, num * keep + v
        top, l = new, following

    lane = lax.broadcasted_iota(jnp.int32, (num.shape[0], STAT), 1)
    stats = jnp.zeros((num.shape[0], STAT), F32)
    for i, term in enumerate(split3(top) + split3(total)):
        stats = jnp.where(lane == i, term, stats)
    for e in range(n):
        at = slice(e * slots, (e + 1) * slots)
        send[e, :, :width] = num[at, :].astype(BF16)
        send[e, :, width:] = stats[at, :].astype(BF16)

    pl.semaphore_wait(barrier, n - 1)
    first = []
    for k, peer in enumerate(peers):
        copy = pltpu.make_async_remote_copy(
            src_ref=send.at[peer],
            dst_ref=recv.at[k],
            send_sem=s1_sem.at[k],
            recv_sem=r1_sem.at[k],
            device_id={"seq": peer},
            device_id_type=MESH,
        )
        copy.start()
        first.append(copy)

    l = logits[...]
    e = jnp.exp(l - jnp.max(l, axis=0, keepdims=True))
    combine_ref[...] = (e / jnp.sum(e, axis=0, keepdims=True)).T.astype(BF16)

    for copy in first:
        copy.wait_recv()
    got = [send[me].astype(F32)] + [recv[k].astype(F32) for k in range(n - 1)]
    terms = [[g[:, width + i : width + i + 1] for i in range(6)] for g in got]
    tops = [t[0] + t[1] + t[2] for t in terms]
    top = functools.reduce(jnp.maximum, tops)
    total = jnp.zeros((slots, 1), F32)
    num = jnp.zeros((slots, width), F32)
    for k in range(n):
        scale = jnp.exp(tops[k] - top)
        total = total + scale * (terms[k][3] + terms[k][4] + terms[k][5])
        num = num + scale * got[k][:, :width]
    slot_in = (num / total).astype(BF16)

    for copy in in_copies + out_copies:
        copy.wait()
    half = ff // 2
    spread_slots(spread, slot_in.astype(F32))
    hidden_m, hidden_v = [], []
    for c in range(0, half, GROUP):
        hidden_v.append(vector_dot(spread, w_in, 0, width, half + c))
        hidden_m.append(jnp.dot(slot_in, w_in[:, c : c + GROUP], preferred_element_type=F32))
    hidden_v = jax.nn.gelu(jnp.concatenate(hidden_v, axis=1)).astype(BF16)
    hidden_m = jax.nn.gelu(jnp.concatenate(hidden_m, axis=1)).astype(BF16)
    spread_slots(spread, hidden_v.astype(F32))
    slot_out = []
    for c in range(0, width, GROUP):
        v = vector_dot(spread, w_out, half, half, c)
        m = jnp.dot(hidden_m, w_out[:half, c : c + GROUP], preferred_element_type=F32)
        slot_out.append(m + v)
    slot_out = jnp.concatenate(slot_out, axis=1)
    gather[me] = slot_out.astype(BF16)

    second = []
    for k, peer in enumerate(peers):
        copy = pltpu.make_async_remote_copy(
            src_ref=gather.at[me],
            dst_ref=gather.at[me],
            send_sem=s2_sem.at[k],
            recv_sem=r2_sem.at[k],
            device_id={"seq": peer},
            device_id_type=MESH,
        )
        copy.start()
        second.append(copy)
    for copy in second:
        copy.wait_recv()
    for e in range(n):
        rows[e * slots : (e + 1) * slots, :] = gather[e].astype(F32)
    slots_ref[...] = rows[...].astype(BF16)
    for copy in first + second:
        copy.wait_send()


def mix_kernel(combine_ref, slots_ref, out_hbm, out, out_sem):
    part = out.shape[0] // MIX_PARTS
    copies = []
    for c in range(MIX_PARTS):
        at = pl.ds(c * part, part)
        out[at, :] = jnp.dot(
            combine_ref[at, :], slots_ref[...], preferred_element_type=F32
        ).astype(BF16)
        copy = pltpu.make_async_copy(out.at[at, :], out_hbm.at[at, :], out_sem.at[c])
        copy.start()
        copies.append(copy)
    for copy in copies:
        copy.wait()


def body(n, tokens, slot_proj, w_in, w_out):
    count, width = tokens.shape
    slots_all = slot_proj.shape[1]
    slots = slots_all // n
    ff = w_in.shape[2]
    assert w_in.shape[0] == 1 and n & (n - 1) == 0
    hbm_spec = pl.BlockSpec(memory_space=pltpu.HBM)
    vmem_spec = pl.BlockSpec(memory_space=pltpu.VMEM)
    wide = width + STAT
    dma = pltpu.SemaphoreType.DMA
    combine, slot_out = pl.pallas_call(
        functools.partial(route_kernel, n),
        out_shape=[
            jax.ShapeDtypeStruct((count, slots_all), BF16),
            jax.ShapeDtypeStruct((slots_all, width), BF16),
        ],
        in_specs=[hbm_spec] * 4,
        out_specs=[vmem_spec] * 2,
        scratch_shapes=[
            pltpu.VMEM((count, width), BF16),
            pltpu.VMEM((slots_all, width), BF16),
            pltpu.VMEM((width, ff), BF16),
            pltpu.VMEM((ff, width), BF16),
            pltpu.VMEM((slots_all, count), F32),
            pltpu.VMEM((n, slots, wide), BF16),
            pltpu.VMEM((n - 1, slots, wide), BF16),
            pltpu.VMEM((n, slots, width), BF16),
            pltpu.VMEM((slots_all, width), F32),
            pltpu.VMEM((slots, max(width, ff // 2), 128), BF16),
            dma((TOKEN_PARTS,)),
            dma,
            dma((FF_PARTS,)),
            dma((FF_PARTS,)),
            dma((n - 1,)),
            dma((n - 1,)),
            dma((n - 1,)),
            dma((n - 1,)),
        ],
        compiler_params=pltpu.CompilerParams(
            collective_id=0, has_side_effects=True, vmem_limit_bytes=48 * 1024 * 1024
        ),
        cost_estimate=pl.CostEstimate(
            flops=4 * count * width * slots_all + 4 * slots * width * ff,
            bytes_accessed=2 * (count * width + 2 * width * ff),
            transcendentals=2 * count * slots_all,
        ),
        name="route",
    )(tokens, pltpu.with_memory_space_constraint(slot_proj.T, pltpu.HBM), w_in, w_out)
    return pl.pallas_call(
        mix_kernel,
        out_shape=jax.ShapeDtypeStruct((count, width), BF16),
        in_specs=[vmem_spec] * 2,
        out_specs=hbm_spec,
        scratch_shapes=[pltpu.VMEM((count, width), BF16), dma((MIX_PARTS,))],
        compiler_params=pltpu.CompilerParams(vmem_limit_bytes=32 * 1024 * 1024),
        cost_estimate=pl.CostEstimate(
            flops=2 * count * width * slots_all,
            bytes_accessed=2 * count * width,
            transcendentals=0,
        ),
        name="mix",
    )(combine, slot_out)


def solution(mesh):
    return jax.shard_map(
        functools.partial(body, mesh.shape["seq"]),
        mesh=mesh,
        in_specs=(P(("clip", "seq"), None), P(), P("seq", None, None), P("seq", None, None)),
        out_specs=P(("clip", "seq"), None),
        check_vma=False,
    )
```

```python
import functools

import jax
import jax.numpy as jnp
from jax import lax
from jax.experimental import pallas as pl
from jax.experimental.pallas import tpu as pltpu
from jax.sharding import PartitionSpec as P

MESH = pl.DeviceIdType.MESH
F32 = jnp.float32
BF16 = jnp.bfloat16
TOKEN_PARTS = 5
MIX_PARTS = 10
GROUP = 256
STAT = 128


def split3(x):
    high = x.astype(BF16).astype(F32)
    middle = (x - high).astype(BF16).astype(F32)
    return [high, middle, x - high - middle]


def spread_slots(spread, x):
    slots, depth = x.shape
    columns = jnp.concatenate([x] * (8 // slots), axis=0).T
    for i in range(slots):
        spread[i, :depth, :] = jnp.broadcast_to(columns[:, i : i + 1], (depth, 128)).astype(BF16)


def vector_dot(spread, w, row, depth, column):
    slots = spread.shape[0]
    sums = [jnp.zeros((16, GROUP), F32) for _ in range(slots)]
    for d in range(0, depth, 64):
        tiles = [w[row + d + r : row + d + r + 16, column : column + GROUP] for r in range(0, 64, 16)]
        for i in range(slots):
            terms = []
            for k, tile in enumerate(tiles):
                value = spread[i, d + 16 * k : d + 16 * k + 16, :]
                terms.append(tile * jnp.concatenate([value] * (GROUP // 128), axis=1))
            pair = (terms[0] + terms[1]) + (terms[2] + terms[3])
            sums[i] = sums[i] + pair.astype(F32)
    return jnp.concatenate([jnp.sum(x, axis=0, keepdims=True) for x in sums], axis=0)


def route_kernel(
    n,
    tokens_hbm,
    proj_hbm,
    w_in_hbm,
    w_out_hbm,
    combine_ref,
    slots_ref,
    tok,
    proj,
    w_in,
    w_out,
    logits,
    send,
    recv,
    gather,
    rows,
    spread,
    tok_sem,
    proj_sem,
    in_sem,
    out_sem,
    s1_sem,
    r1_sem,
    s2_sem,
    r2_sem,
):
    me = lax.axis_index("seq")
    width = tok.shape[1]
    slots = send.shape[1]
    part = tok.shape[0] // TOKEN_PARTS
    ff = w_in.shape[1]

    proj_copy = pltpu.make_async_copy(proj_hbm, proj, proj_sem)
    proj_copy.start()
    tok_copies = []
    for c in range(TOKEN_PARTS):
        at = pl.ds(c * part, part)
        copy = pltpu.make_async_copy(tokens_hbm.at[at, :], tok.at[at, :], tok_sem.at[c])
        copy.start()
        tok_copies.append(copy)
    in_copies, out_copies = [], []
    for c in range(TOKEN_PARTS):
        at = pl.ds(c * (width // TOKEN_PARTS), width // TOKEN_PARTS)
        in_copies.append(pltpu.make_async_copy(w_in_hbm.at[0, at, :], w_in.at[at, :], in_sem.at[c]))
        at = pl.ds(c * (ff // TOKEN_PARTS), ff // TOKEN_PARTS)
        out_copies.append(pltpu.make_async_copy(w_out_hbm.at[0, at, :], w_out.at[at, :], out_sem.at[c]))

    barrier = pltpu.get_barrier_semaphore()
    peers = [lax.bitwise_xor(me, n - 1 - k) for k in range(n - 1)]
    for peer in peers:
        pl.semaphore_signal(barrier, inc=1, device_id={"seq": peer}, device_id_type=MESH)

    proj_copy.wait()
    proj_cols = proj[...].T

    def part_logits(c):
        tok_copies[c].wait()
        in_copies[c].start()
        out_copies[c].start()
        at = slice(c * part, (c + 1) * part)
        l = jnp.dot(tok[at, :], proj_cols, preferred_element_type=F32).T
        logits[:, at] = l
        return l

    top = total = num = None
    l = part_logits(0)
    for c in range(TOKEN_PARTS):
        if c + 1 < TOKEN_PARTS:
            following = part_logits(c + 1)
        here = jnp.max(l, axis=1, keepdims=True)
        new = here if c == 0 else jnp.maximum(top, here)
        shifted = jnp.exp(l - new)
        t = jnp.sum(shifted, axis=1, keepdims=True)
        x = tok[c * part : (c + 1) * part, :]
        v = jnp.dot(shifted.astype(BF16), x, preferred_element_type=F32)
        if c == 0:
            total, num = t, v
        else:
            keep = jnp.exp(top - new)
            total, num = total * keep + t, num * keep + v
        top, l = new, following

    lane = lax.broadcasted_iota(jnp.int32, (num.shape[0], STAT), 1)
    stats = jnp.zeros((num.shape[0], STAT), F32)
    for i, term in enumerate(split3(top) + split3(total)):
        stats = jnp.where(lane == i, term, stats)
    for e in range(n):
        at = slice(e * slots, (e + 1) * slots)
        send[e, :, :width] = num[at, :].astype(BF16)
        send[e, :, width:] = stats[at, :].astype(BF16)

    pl.semaphore_wait(barrier, n - 1)
    first = []
    for k, peer in enumerate(peers):
        copy = pltpu.make_async_remote_copy(
            src_ref=send.at[peer],
            dst_ref=recv.at[k],
            send_sem=s1_sem.at[k],
            recv_sem=r1_sem.at[k],
            device_id={"seq": peer},
            device_id_type=MESH,
        )
        copy.start()
        first.append(copy)

    l = logits[...]
    e = jnp.exp(l - jnp.max(l, axis=0, keepdims=True))
    combine_ref[...] = (e / jnp.sum(e, axis=0, keepdims=True)).T.astype(BF16)

    for copy in first:
        copy.wait_recv()
    got = [send[me].astype(F32)] + [recv[k].astype(F32) for k in range(n - 1)]
    terms = [[g[:, width + i : width + i + 1] for i in range(6)] for g in got]
    tops = [t[0] + t[1] + t[2] for t in terms]
    top = functools.reduce(jnp.maximum, tops)
    total = jnp.zeros((slots, 1), F32)
    num = jnp.zeros((slots, width), F32)
    for k in range(n):
        scale = jnp.exp(tops[k] - top)
        total = total + scale * (terms[k][3] + terms[k][4] + terms[k][5])
        num = num + scale * got[k][:, :width]
    slot_in = (num / total).astype(BF16)

    for copy in in_copies + out_copies:
        copy.wait()
    half = ff // 2
    spread_slots(spread, slot_in.astype(F32))
    hidden_m, hidden_v = [], []
    for c in range(0, half, GROUP):
        hidden_v.append(vector_dot(spread, w_in, 0, width, half + c))
        hidden_m.append(jnp.dot(slot_in, w_in[:, c : c + GROUP], preferred_element_type=F32))
    hidden_v = jax.nn.gelu(jnp.concatenate(hidden_v, axis=1)).astype(BF16)
    hidden_m = jax.nn.gelu(jnp.concatenate(hidden_m, axis=1)).astype(BF16)
    spread_slots(spread, hidden_v.astype(F32))
    slot_out = []
    for c in range(0, width, GROUP):
        v = vector_dot(spread, w_out, half, half, c)
        m = jnp.dot(hidden_m, w_out[:half, c : c + GROUP], preferred_element_type=F32)
        slot_out.append(m + v)
    slot_out = jnp.concatenate(slot_out, axis=1)
    gather[me] = slot_out.astype(BF16)

    second = []
    for k, peer in enumerate(peers):
        copy = pltpu.make_async_remote_copy(
            src_ref=gather.at[me],
            dst_ref=gather.at[me],
            send_sem=s2_sem.at[k],
            recv_sem=r2_sem.at[k],
            device_id={"seq": peer},
            device_id_type=MESH,
        )
        copy.start()
        second.append(copy)
    for copy in second:
        copy.wait_recv()
    for e in range(n):
        rows[e * slots : (e + 1) * slots, :] = gather[e].astype(F32)
    slots_ref[...] = rows[...].astype(BF16)
    for copy in first + second:
        copy.wait_send()


def mix_kernel(combine_ref, slots_ref, out_hbm, out, out_sem):
    part = out.shape[0] // MIX_PARTS
    copies = []
    for c in range(MIX_PARTS):
        at = pl.ds(c * part, part)
        out[at, :] = jnp.dot(
            combine_ref[at, :], slots_ref[...], preferred_element_type=F32
        ).astype(BF16)
        copy = pltpu.make_async_copy(out.at[at, :], out_hbm.at[at, :], out_sem.at[c])
        copy.start()
        copies.append(copy)
    for copy in copies:
        copy.wait()


def body(n, tokens, slot_proj, w_in, w_out):
    count, width = tokens.shape
    slots_all = slot_proj.shape[1]
    slots = slots_all // n
    ff = w_in.shape[2]
    assert w_in.shape[0] == 1 and n & (n - 1) == 0
    hbm_spec = pl.BlockSpec(memory_space=pltpu.HBM)
    vmem_spec = pl.BlockSpec(memory_space=pltpu.VMEM)
    wide = width + STAT
    dma = pltpu.SemaphoreType.DMA
    combine, slot_out = pl.pallas_call(
        functools.partial(route_kernel, n),
        out_shape=[
            jax.ShapeDtypeStruct((count, slots_all), BF16),
            jax.ShapeDtypeStruct((slots_all, width), BF16),
        ],
        in_specs=[hbm_spec] * 4,
        out_specs=[vmem_spec] * 2,
        scratch_shapes=[
            pltpu.VMEM((count, width), BF16),
            pltpu.VMEM((slots_all, width), BF16),
            pltpu.VMEM((width, ff), BF16),
            pltpu.VMEM((ff, width), BF16),
            pltpu.VMEM((slots_all, count), F32),
            pltpu.VMEM((n, slots, wide), BF16),
            pltpu.VMEM((n - 1, slots, wide), BF16),
            pltpu.VMEM((n, slots, width), BF16),
            pltpu.VMEM((slots_all, width), F32),
            pltpu.VMEM((slots, max(width, ff // 2), 128), BF16),
            dma((TOKEN_PARTS,)),
            dma,
            dma((TOKEN_PARTS,)),
            dma((TOKEN_PARTS,)),
            dma((n - 1,)),
            dma((n - 1,)),
            dma((n - 1,)),
            dma((n - 1,)),
        ],
        compiler_params=pltpu.CompilerParams(
            collective_id=0, has_side_effects=True, vmem_limit_bytes=48 * 1024 * 1024
        ),
        cost_estimate=pl.CostEstimate(
            flops=4 * count * width * slots_all + 4 * slots * width * ff,
            bytes_accessed=2 * (count * width + 2 * width * ff),
            transcendentals=2 * count * slots_all,
        ),
        name="route",
    )(tokens, pltpu.with_memory_space_constraint(slot_proj.T, pltpu.HBM), w_in, w_out)
    return pl.pallas_call(
        mix_kernel,
        out_shape=jax.ShapeDtypeStruct((count, width), BF16),
        in_specs=[vmem_spec] * 2,
        out_specs=hbm_spec,
        scratch_shapes=[pltpu.VMEM((count, width), BF16), dma((MIX_PARTS,))],
        compiler_params=pltpu.CompilerParams(vmem_limit_bytes=32 * 1024 * 1024),
        cost_estimate=pl.CostEstimate(
            flops=2 * count * width * slots_all,
            bytes_accessed=2 * count * width,
            transcendentals=0,
        ),
        name="mix",
    )(combine, slot_out)


def solution(mesh):
    return jax.shard_map(
        functools.partial(body, mesh.shape["seq"]),
        mesh=mesh,
        in_specs=(P(("clip", "seq"), None), P(), P("seq", None, None), P("seq", None, None)),
        out_specs=P(("clip", "seq"), None),
        check_vma=False,
    )
```

```python
import functools

import jax
import jax.numpy as jnp
from jax import lax
from jax.experimental import pallas as pl
from jax.experimental.pallas import tpu as pltpu
from jax.sharding import PartitionSpec as P

MESH = pl.DeviceIdType.MESH
F32 = jnp.float32
BF16 = jnp.bfloat16
TOKEN_PARTS = 5
MIX_PARTS = 10
GROUP = 256
STAT = 128


def split3(x):
    high = x.astype(BF16).astype(F32)
    middle = (x - high).astype(BF16).astype(F32)
    return [high, middle, x - high - middle]


def spread_slots(spread, x):
    slots, depth = x.shape
    columns = jnp.concatenate([x] * (8 // slots), axis=0).T
    for i in range(slots):
        spread[i, :depth, :] = jnp.broadcast_to(columns[:, i : i + 1], (depth, 128)).astype(BF16)


def vector_dot(spread, w, row, depth, column):
    slots = spread.shape[0]
    sums = [jnp.zeros((16, GROUP), F32) for _ in range(slots)]
    for d in range(0, depth, 64):
        tiles = [w[row + d + r : row + d + r + 16, column : column + GROUP] for r in range(0, 64, 16)]
        for i in range(slots):
            terms = []
            for k, tile in enumerate(tiles):
                value = spread[i, d + 16 * k : d + 16 * k + 16, :]
                terms.append(tile * jnp.concatenate([value] * (GROUP // 128), axis=1))
            pair = (terms[0] + terms[1]) + (terms[2] + terms[3])
            sums[i] = sums[i] + pair.astype(F32)
    return jnp.concatenate([jnp.sum(x, axis=0, keepdims=True) for x in sums], axis=0)


def route_kernel(
    n,
    tokens_hbm,
    proj_hbm,
    w_in_hbm,
    w_out_hbm,
    combine_ref,
    slots_ref,
    tok,
    proj,
    w_in,
    w_out,
    logits,
    send,
    recv,
    gather,
    rows,
    spread,
    tok_sem,
    proj_sem,
    in_sem,
    out_sem,
    s1_sem,
    r1_sem,
    s2_sem,
    r2_sem,
):
    me = lax.axis_index("seq")
    width = tok.shape[1]
    slots = send.shape[1]
    part = tok.shape[0] // TOKEN_PARTS
    ff = w_in.shape[1]

    proj_copy = pltpu.make_async_copy(proj_hbm, proj, proj_sem)
    proj_copy.start()
    tok_copies = []
    for c in range(TOKEN_PARTS):
        at = pl.ds(c * part, part)
        copy = pltpu.make_async_copy(tokens_hbm.at[at, :], tok.at[at, :], tok_sem.at[c])
        copy.start()
        tok_copies.append(copy)
    in_copies, out_copies = [], []
    for c in range(TOKEN_PARTS):
        at = pl.ds(c * (width // TOKEN_PARTS), width // TOKEN_PARTS)
        in_copies.append(pltpu.make_async_copy(w_in_hbm.at[0, at, :], w_in.at[at, :], in_sem.at[c]))
        at = pl.ds(c * (ff // TOKEN_PARTS), ff // TOKEN_PARTS)
        out_copies.append(pltpu.make_async_copy(w_out_hbm.at[0, at, :], w_out.at[at, :], out_sem.at[c]))

    barrier = pltpu.get_barrier_semaphore()
    peers = [lax.bitwise_xor(me, n - 1 - k) for k in range(n - 1)]
    for peer in peers:
        pl.semaphore_signal(barrier, inc=1, device_id={"seq": peer}, device_id_type=MESH)

    proj_copy.wait()

    def part_logits(c):
        tok_copies[c].wait()
        in_copies[c].start()
        out_copies[c].start()
        at = slice(c * part, (c + 1) * part)
        l = lax.dot_general(
            proj[...], tok[at, :], (((1,), (1,)), ((), ())), preferred_element_type=F32
        )
        logits[:, at] = l
        return l

    top = total = num = None
    l = part_logits(0)
    for c in range(TOKEN_PARTS):
        if c + 1 < TOKEN_PARTS:
            following = part_logits(c + 1)
        here = jnp.max(l, axis=1, keepdims=True)
        new = here if c == 0 else jnp.maximum(top, here)
        shifted = jnp.exp(l - new)
        t = jnp.sum(shifted, axis=1, keepdims=True)
        x = tok[c * part : (c + 1) * part, :]
        v = jnp.dot(shifted.astype(BF16), x, preferred_element_type=F32)
        if c == 0:
            total, num = t, v
        else:
            keep = jnp.exp(top - new)
            total, num = total * keep + t, num * keep + v
        top, l = new, following

    lane = lax.broadcasted_iota(jnp.int32, (num.shape[0], STAT), 1)
    stats = jnp.zeros((num.shape[0], STAT), F32)
    for i, term in enumerate(split3(top) + split3(total)):
        stats = jnp.where(lane == i, term, stats)
    for e in range(n):
        at = slice(e * slots, (e + 1) * slots)
        send[e, :, :width] = num[at, :].astype(BF16)
        send[e, :, width:] = stats[at, :].astype(BF16)

    pl.semaphore_wait(barrier, n - 1)
    first = []
    for k, peer in enumerate(peers):
        copy = pltpu.make_async_remote_copy(
            src_ref=send.at[peer],
            dst_ref=recv.at[k],
            send_sem=s1_sem.at[k],
            recv_sem=r1_sem.at[k],
            device_id={"seq": peer},
            device_id_type=MESH,
        )
        copy.start()
        first.append(copy)

    l = logits[...]
    e = jnp.exp(l - jnp.max(l, axis=0, keepdims=True))
    combine_ref[...] = (e / jnp.sum(e, axis=0, keepdims=True)).T.astype(BF16)

    for copy in first:
        copy.wait_recv()
    got = [send[me].astype(F32)] + [recv[k].astype(F32) for k in range(n - 1)]
    terms = [[g[:, width + i : width + i + 1] for i in range(6)] for g in got]
    tops = [t[0] + t[1] + t[2] for t in terms]
    top = functools.reduce(jnp.maximum, tops)
    total = jnp.zeros((slots, 1), F32)
    num = jnp.zeros((slots, width), F32)
    for k in range(n):
        scale = jnp.exp(tops[k] - top)
        total = total + scale * (terms[k][3] + terms[k][4] + terms[k][5])
        num = num + scale * got[k][:, :width]
    slot_in = (num / total).astype(BF16)

    for copy in in_copies + out_copies:
        copy.wait()
    half = ff // 2
    spread_slots(spread, slot_in.astype(F32))
    hidden_m, hidden_v = [], []
    for c in range(0, half, GROUP):
        hidden_v.append(vector_dot(spread, w_in, 0, width, half + c))
        hidden_m.append(jnp.dot(slot_in, w_in[:, c : c + GROUP], preferred_element_type=F32))
    hidden_v = jax.nn.gelu(jnp.concatenate(hidden_v, axis=1)).astype(BF16)
    hidden_m = jax.nn.gelu(jnp.concatenate(hidden_m, axis=1)).astype(BF16)
    spread_slots(spread, hidden_v.astype(F32))
    slot_out = []
    for c in range(0, width, GROUP):
        v = vector_dot(spread, w_out, half, half, c)
        m = jnp.dot(hidden_m, w_out[:half, c : c + GROUP], preferred_element_type=F32)
        slot_out.append(m + v)
    slot_out = jnp.concatenate(slot_out, axis=1)
    gather[me] = slot_out.astype(BF16)

    second = []
    for k, peer in enumerate(peers):
        copy = pltpu.make_async_remote_copy(
            src_ref=gather.at[me],
            dst_ref=gather.at[me],
            send_sem=s2_sem.at[k],
            recv_sem=r2_sem.at[k],
            device_id={"seq": peer},
            device_id_type=MESH,
        )
        copy.start()
        second.append(copy)
    for copy in second:
        copy.wait_recv()
    for e in range(n):
        rows[e * slots : (e + 1) * slots, :] = gather[e].astype(F32)
    slots_ref[...] = rows[...].astype(BF16)
    for copy in first + second:
        copy.wait_send()


def mix_kernel(combine_ref, slots_ref, out_hbm, out, out_sem):
    part = out.shape[0] // MIX_PARTS
    copies = []
    for c in range(MIX_PARTS):
        at = pl.ds(c * part, part)
        out[at, :] = jnp.dot(
            combine_ref[at, :], slots_ref[...], preferred_element_type=F32
        ).astype(BF16)
        copy = pltpu.make_async_copy(out.at[at, :], out_hbm.at[at, :], out_sem.at[c])
        copy.start()
        copies.append(copy)
    for copy in copies:
        copy.wait()


def body(n, tokens, slot_proj, w_in, w_out):
    count, width = tokens.shape
    slots_all = slot_proj.shape[1]
    slots = slots_all // n
    ff = w_in.shape[2]
    assert w_in.shape[0] == 1 and n & (n - 1) == 0
    hbm_spec = pl.BlockSpec(memory_space=pltpu.HBM)
    vmem_spec = pl.BlockSpec(memory_space=pltpu.VMEM)
    wide = width + STAT
    dma = pltpu.SemaphoreType.DMA
    combine, slot_out = pl.pallas_call(
        functools.partial(route_kernel, n),
        out_shape=[
            jax.ShapeDtypeStruct((count, slots_all), BF16),
            jax.ShapeDtypeStruct((slots_all, width), BF16),
        ],
        in_specs=[hbm_spec] * 4,
        out_specs=[vmem_spec] * 2,
        scratch_shapes=[
            pltpu.VMEM((count, width), BF16),
            pltpu.VMEM((slots_all, width), BF16),
            pltpu.VMEM((width, ff), BF16),
            pltpu.VMEM((ff, width), BF16),
            pltpu.VMEM((slots_all, count), F32),
            pltpu.VMEM((n, slots, wide), BF16),
            pltpu.VMEM((n - 1, slots, wide), BF16),
            pltpu.VMEM((n, slots, width), BF16),
            pltpu.VMEM((slots_all, width), F32),
            pltpu.VMEM((slots, max(width, ff // 2), 128), BF16),
            dma((TOKEN_PARTS,)),
            dma,
            dma((TOKEN_PARTS,)),
            dma((TOKEN_PARTS,)),
            dma((n - 1,)),
            dma((n - 1,)),
            dma((n - 1,)),
            dma((n - 1,)),
        ],
        compiler_params=pltpu.CompilerParams(
            collective_id=0, has_side_effects=True, vmem_limit_bytes=48 * 1024 * 1024
        ),
        cost_estimate=pl.CostEstimate(
            flops=4 * count * width * slots_all + 4 * slots * width * ff,
            bytes_accessed=2 * (count * width + 2 * width * ff),
            transcendentals=2 * count * slots_all,
        ),
        name="route",
    )(tokens, pltpu.with_memory_space_constraint(slot_proj.T, pltpu.HBM), w_in, w_out)
    return pl.pallas_call(
        mix_kernel,
        out_shape=jax.ShapeDtypeStruct((count, width), BF16),
        in_specs=[vmem_spec] * 2,
        out_specs=hbm_spec,
        scratch_shapes=[pltpu.VMEM((count, width), BF16), dma((MIX_PARTS,))],
        compiler_params=pltpu.CompilerParams(vmem_limit_bytes=32 * 1024 * 1024),
        cost_estimate=pl.CostEstimate(
            flops=2 * count * width * slots_all,
            bytes_accessed=2 * count * width,
            transcendentals=0,
        ),
        name="mix",
    )(combine, slot_out)


def solution(mesh):
    return jax.shard_map(
        functools.partial(body, mesh.shape["seq"]),
        mesh=mesh,
        in_specs=(P(("clip", "seq"), None), P(), P("seq", None, None), P("seq", None, None)),
        out_specs=P(("clip", "seq"), None),
        check_vma=False,
    )
```

```python
import functools

import jax
import jax.numpy as jnp
from jax import lax
from jax.experimental import pallas as pl
from jax.experimental.pallas import tpu as pltpu
from jax.sharding import PartitionSpec as P

MESH = pl.DeviceIdType.MESH
F32 = jnp.float32
BF16 = jnp.bfloat16
TOKEN_PARTS = 5
MIX_PARTS = 10
FF_PART = 512
STAT = 128


def split3(x):
    high = x.astype(BF16).astype(F32)
    middle = (x - high).astype(BF16).astype(F32)
    return [high, middle, x - high - middle]


def route_kernel(
    n,
    tokens_hbm,
    proj_hbm,
    w_in_hbm,
    w_out_hbm,
    combine_ref,
    slots_ref,
    tok,
    proj,
    w_in,
    w_out,
    logits,
    send,
    recv,
    gather,
    rows,
    tok_sem,
    proj_sem,
    in_sem,
    out_sem,
    s1_sem,
    r1_sem,
    s2_sem,
    r2_sem,
):
    me = lax.axis_index("seq")
    width = tok.shape[1]
    slots = send.shape[1]
    part = tok.shape[0] // TOKEN_PARTS
    ff = w_in.shape[1]

    proj_copy = pltpu.make_async_copy(proj_hbm, proj, proj_sem)
    proj_copy.start()
    tok_copies = []
    for c in range(TOKEN_PARTS):
        at = pl.ds(c * part, part)
        copy = pltpu.make_async_copy(tokens_hbm.at[at, :], tok.at[at, :], tok_sem.at[c])
        copy.start()
        tok_copies.append(copy)
    in_copies, out_copies = [], []
    for c in range(TOKEN_PARTS):
        at = pl.ds(c * (width // TOKEN_PARTS), width // TOKEN_PARTS)
        in_copies.append(pltpu.make_async_copy(w_in_hbm.at[0, at, :], w_in.at[at, :], in_sem.at[c]))
        at = pl.ds(c * (ff // TOKEN_PARTS), ff // TOKEN_PARTS)
        out_copies.append(pltpu.make_async_copy(w_out_hbm.at[0, at, :], w_out.at[at, :], out_sem.at[c]))

    barrier = pltpu.get_barrier_semaphore()
    peers = [lax.bitwise_xor(me, n - 1 - k) for k in range(n - 1)]
    for peer in peers:
        pl.semaphore_signal(barrier, inc=1, device_id={"seq": peer}, device_id_type=MESH)

    proj_copy.wait()

    def part_logits(c):
        tok_copies[c].wait()
        in_copies[c].start()
        out_copies[c].start()
        at = slice(c * part, (c + 1) * part)
        l = lax.dot_general(
            proj[...], tok[at, :], (((1,), (1,)), ((), ())), preferred_element_type=F32
        )
        logits[:, at] = l
        return l

    top = total = num = None
    l = part_logits(0)
    for c in range(TOKEN_PARTS):
        if c + 1 < TOKEN_PARTS:
            following = part_logits(c + 1)
        here = jnp.max(l, axis=1, keepdims=True)
        new = here if c == 0 else jnp.maximum(top, here)
        shifted = jnp.exp(l - new)
        t = jnp.sum(shifted, axis=1, keepdims=True)
        x = tok[c * part : (c + 1) * part, :]
        v = jnp.dot(shifted.astype(BF16), x, preferred_element_type=F32)
        if c == 0:
            total, num = t, v
        else:
            keep = jnp.exp(top - new)
            total, num = total * keep + t, num * keep + v
        top, l = new, following

    lane = lax.broadcasted_iota(jnp.int32, (num.shape[0], STAT), 1)
    stats = jnp.zeros((num.shape[0], STAT), F32)
    for i, term in enumerate(split3(top) + split3(total)):
        stats = jnp.where(lane == i, term, stats)
    for e in range(n):
        at = slice(e * slots, (e + 1) * slots)
        send[e, :, :width] = num[at, :].astype(BF16)
        send[e, :, width:] = stats[at, :].astype(BF16)

    pl.semaphore_wait(barrier, n - 1)
    first = []
    for k, peer in enumerate(peers):
        copy = pltpu.make_async_remote_copy(
            src_ref=send.at[peer],
            dst_ref=recv.at[k],
            send_sem=s1_sem.at[k],
            recv_sem=r1_sem.at[k],
            device_id={"seq": peer},
            device_id_type=MESH,
        )
        copy.start()
        first.append(copy)

    l = logits[...]
    e = jnp.exp(l - jnp.max(l, axis=0, keepdims=True))
    combine_ref[...] = (e / jnp.sum(e, axis=0, keepdims=True)).T.astype(BF16)

    for copy in first:
        copy.wait_recv()
    got = [send[me].astype(F32)] + [recv[k].astype(F32) for k in range(n - 1)]
    terms = [[g[:, width + i : width + i + 1] for i in range(6)] for g in got]
    tops = [t[0] + t[1] + t[2] for t in terms]
    top = functools.reduce(jnp.maximum, tops)
    total = jnp.zeros((slots, 1), F32)
    num = jnp.zeros((slots, width), F32)
    for k in range(n):
        scale = jnp.exp(tops[k] - top)
        total = total + scale * (terms[k][3] + terms[k][4] + terms[k][5])
        num = num + scale * got[k][:, :width]
    slot_in = (num / total).astype(BF16)

    for copy in in_copies + out_copies:
        copy.wait()
    def first_product(c):
        h = jnp.dot(slot_in, w_in[:, c : c + FF_PART], preferred_element_type=F32)
        return jax.nn.gelu(h).astype(BF16)

    slot_out = jnp.zeros((slots, width), F32)
    hidden = first_product(0)
    for c in range(0, ff, FF_PART):
        later = first_product(c + FF_PART) if c + FF_PART < ff else None
        slot_out = slot_out + jnp.dot(
            hidden, w_out[c : c + FF_PART, :], preferred_element_type=F32
        )
        hidden = later
    gather[me] = slot_out.astype(BF16)

    second = []
    for k, peer in enumerate(peers):
        copy = pltpu.make_async_remote_copy(
            src_ref=gather.at[me],
            dst_ref=gather.at[me],
            send_sem=s2_sem.at[k],
            recv_sem=r2_sem.at[k],
            device_id={"seq": peer},
            device_id_type=MESH,
        )
        copy.start()
        second.append(copy)
    for copy in second:
        copy.wait_recv()
    for e in range(n):
        rows[e * slots : (e + 1) * slots, :] = gather[e].astype(F32)
    slots_ref[...] = rows[...].astype(BF16)
    for copy in first + second:
        copy.wait_send()


def mix_kernel(combine_ref, slots_ref, out_hbm, out, out_sem):
    part = out.shape[0] // MIX_PARTS
    copies = []
    for c in range(MIX_PARTS):
        at = pl.ds(c * part, part)
        out[at, :] = jnp.dot(
            combine_ref[at, :], slots_ref[...], preferred_element_type=F32
        ).astype(BF16)
        copy = pltpu.make_async_copy(out.at[at, :], out_hbm.at[at, :], out_sem.at[c])
        copy.start()
        copies.append(copy)
    for copy in copies:
        copy.wait()


def body(n, tokens, slot_proj, w_in, w_out):
    count, width = tokens.shape
    slots_all = slot_proj.shape[1]
    slots = slots_all // n
    ff = w_in.shape[2]
    assert w_in.shape[0] == 1 and n & (n - 1) == 0
    hbm_spec = pl.BlockSpec(memory_space=pltpu.HBM)
    vmem_spec = pl.BlockSpec(memory_space=pltpu.VMEM)
    wide = width + STAT
    dma = pltpu.SemaphoreType.DMA
    combine, slot_out = pl.pallas_call(
        functools.partial(route_kernel, n),
        out_shape=[
            jax.ShapeDtypeStruct((count, slots_all), BF16),
            jax.ShapeDtypeStruct((slots_all, width), BF16),
        ],
        in_specs=[hbm_spec] * 4,
        out_specs=[vmem_spec] * 2,
        scratch_shapes=[
            pltpu.VMEM((count, width), BF16),
            pltpu.VMEM((slots_all, width), BF16),
            pltpu.VMEM((width, ff), BF16),
            pltpu.VMEM((ff, width), BF16),
            pltpu.VMEM((slots_all, count), F32),
            pltpu.VMEM((n, slots, wide), BF16),
            pltpu.VMEM((n - 1, slots, wide), BF16),
            pltpu.VMEM((n, slots, width), BF16),
            pltpu.VMEM((slots_all, width), F32),
            dma((TOKEN_PARTS,)),
            dma,
            dma((TOKEN_PARTS,)),
            dma((TOKEN_PARTS,)),
            dma((n - 1,)),
            dma((n - 1,)),
            dma((n - 1,)),
            dma((n - 1,)),
        ],
        compiler_params=pltpu.CompilerParams(
            collective_id=0, has_side_effects=True, vmem_limit_bytes=48 * 1024 * 1024
        ),
        cost_estimate=pl.CostEstimate(
            flops=4 * count * width * slots_all + 4 * slots * width * ff,
            bytes_accessed=2 * (count * width + 2 * width * ff),
            transcendentals=2 * count * slots_all,
        ),
        name="route",
    )(tokens, pltpu.with_memory_space_constraint(slot_proj.T, pltpu.HBM), w_in, w_out)
    return pl.pallas_call(
        mix_kernel,
        out_shape=jax.ShapeDtypeStruct((count, width), BF16),
        in_specs=[vmem_spec] * 2,
        out_specs=hbm_spec,
        scratch_shapes=[pltpu.VMEM((count, width), BF16), dma((MIX_PARTS,))],
        compiler_params=pltpu.CompilerParams(vmem_limit_bytes=32 * 1024 * 1024),
        cost_estimate=pl.CostEstimate(
            flops=2 * count * width * slots_all,
            bytes_accessed=2 * count * width,
            transcendentals=0,
        ),
        name="mix",
    )(combine, slot_out)


def solution(mesh):
    return jax.shard_map(
        functools.partial(body, mesh.shape["seq"]),
        mesh=mesh,
        in_specs=(P(("clip", "seq"), None), P(), P("seq", None, None), P("seq", None, None)),
        out_specs=P(("clip", "seq"), None),
        check_vma=False,
    )
```

```python
import functools

import jax
import jax.numpy as jnp
from jax import lax
from jax.experimental import pallas as pl
from jax.experimental.pallas import tpu as pltpu
from jax.sharding import PartitionSpec as P

MESH = pl.DeviceIdType.MESH
F32 = jnp.float32
BF16 = jnp.bfloat16
TOKEN_PARTS = 5
MIX_PARTS = 10
STAT = 128


def split3(x):
    high = x.astype(BF16).astype(F32)
    middle = (x - high).astype(BF16).astype(F32)
    return [high, middle, x - high - middle]


def route_kernel(
    n,
    tokens_hbm,
    proj_hbm,
    w_in_hbm,
    w_out_hbm,
    combine_ref,
    slots_ref,
    tok,
    proj,
    w_in,
    w_out,
    logits,
    send,
    recv,
    gather,
    rows,
    tok_sem,
    proj_sem,
    in_sem,
    out_sem,
    s1_sem,
    r1_sem,
    s2_sem,
    r2_sem,
):
    me = lax.axis_index("seq")
    width = tok.shape[1]
    slots = send.shape[1]
    part = tok.shape[0] // TOKEN_PARTS
    ff = w_in.shape[1]

    proj_copy = pltpu.make_async_copy(proj_hbm, proj, proj_sem)
    proj_copy.start()
    tok_copies = []
    for c in range(TOKEN_PARTS):
        at = pl.ds(c * part, part)
        copy = pltpu.make_async_copy(tokens_hbm.at[at, :], tok.at[at, :], tok_sem.at[c])
        copy.start()
        tok_copies.append(copy)
    in_copies, out_copies = [], []
    for c in range(TOKEN_PARTS):
        at = pl.ds(c * (width // TOKEN_PARTS), width // TOKEN_PARTS)
        in_copies.append(pltpu.make_async_copy(w_in_hbm.at[0, at, :], w_in.at[at, :], in_sem.at[c]))
        at = pl.ds(c * (ff // TOKEN_PARTS), ff // TOKEN_PARTS)
        out_copies.append(pltpu.make_async_copy(w_out_hbm.at[0, at, :], w_out.at[at, :], out_sem.at[c]))

    barrier = pltpu.get_barrier_semaphore()
    peers = [lax.bitwise_xor(me, n - 1 - k) for k in range(n - 1)]
    for peer in peers:
        pl.semaphore_signal(barrier, inc=1, device_id={"seq": peer}, device_id_type=MESH)

    proj_copy.wait()

    def part_logits(c):
        tok_copies[c].wait()
        for copy in (in_copies + out_copies)[2 * c : 2 * c + 2]:
            copy.start()
        at = slice(c * part, (c + 1) * part)
        l = lax.dot_general(
            proj[...], tok[at, :], (((1,), (1,)), ((), ())), preferred_element_type=F32
        )
        logits[:, at] = l
        return l

    top = total = num = None
    l = part_logits(0)
    for c in range(TOKEN_PARTS):
        if c + 1 < TOKEN_PARTS:
            following = part_logits(c + 1)
        here = jnp.max(l, axis=1, keepdims=True)
        new = here if c == 0 else jnp.maximum(top, here)
        shifted = jnp.exp(l - new)
        t = jnp.sum(shifted, axis=1, keepdims=True)
        x = tok[c * part : (c + 1) * part, :]
        v = jnp.dot(shifted.astype(BF16), x, preferred_element_type=F32)
        if c == 0:
            total, num = t, v
        else:
            keep = jnp.exp(top - new)
            total, num = total * keep + t, num * keep + v
        top, l = new, following

    lane = lax.broadcasted_iota(jnp.int32, (num.shape[0], STAT), 1)
    stats = jnp.zeros((num.shape[0], STAT), F32)
    for i, term in enumerate(split3(top) + split3(total)):
        stats = jnp.where(lane == i, term, stats)
    for e in range(n):
        at = slice(e * slots, (e + 1) * slots)
        send[e, :, :width] = num[at, :].astype(BF16)
        send[e, :, width:] = stats[at, :].astype(BF16)

    pl.semaphore_wait(barrier, n - 1)
    first = []
    for k, peer in enumerate(peers):
        copy = pltpu.make_async_remote_copy(
            src_ref=send.at[peer],
            dst_ref=recv.at[k],
            send_sem=s1_sem.at[k],
            recv_sem=r1_sem.at[k],
            device_id={"seq": peer},
            device_id_type=MESH,
        )
        copy.start()
        first.append(copy)

    l = logits[...]
    e = jnp.exp(l - jnp.max(l, axis=0, keepdims=True))
    combine_ref[...] = (e / jnp.sum(e, axis=0, keepdims=True)).T.astype(BF16)

    for copy in first:
        copy.wait_recv()
    got = [send[me].astype(F32)] + [recv[k].astype(F32) for k in range(n - 1)]
    terms = [[g[:, width + i : width + i + 1] for i in range(6)] for g in got]
    tops = [t[0] + t[1] + t[2] for t in terms]
    top = functools.reduce(jnp.maximum, tops)
    total = jnp.zeros((slots, 1), F32)
    num = jnp.zeros((slots, width), F32)
    for k in range(n):
        scale = jnp.exp(tops[k] - top)
        total = total + scale * (terms[k][3] + terms[k][4] + terms[k][5])
        num = num + scale * got[k][:, :width]
    slot_in = (num / total).astype(BF16)

    hidden = jnp.zeros((slots, ff), F32)
    for c in range(TOKEN_PARTS):
        at = slice(c * (width // TOKEN_PARTS), (c + 1) * (width // TOKEN_PARTS))
        in_copies[c].wait()
        hidden = hidden + jnp.dot(slot_in[:, at], w_in[at, :], preferred_element_type=F32)
    hidden = jax.nn.gelu(hidden).astype(BF16)
    slot_out = jnp.zeros((slots, width), F32)
    for c in range(TOKEN_PARTS):
        at = slice(c * (ff // TOKEN_PARTS), (c + 1) * (ff // TOKEN_PARTS))
        out_copies[c].wait()
        slot_out = slot_out + jnp.dot(hidden[:, at], w_out[at, :], preferred_element_type=F32)
    gather[me] = slot_out.astype(BF16)

    second = []
    for k, peer in enumerate(peers):
        copy = pltpu.make_async_remote_copy(
            src_ref=gather.at[me],
            dst_ref=gather.at[me],
            send_sem=s2_sem.at[k],
            recv_sem=r2_sem.at[k],
            device_id={"seq": peer},
            device_id_type=MESH,
        )
        copy.start()
        second.append(copy)
    for copy in second:
        copy.wait_recv()
    for e in range(n):
        rows[e * slots : (e + 1) * slots, :] = gather[e].astype(F32)
    slots_ref[...] = rows[...].astype(BF16)
    for copy in first + second:
        copy.wait_send()


def mix_kernel(combine_ref, slots_ref, out_hbm, out, out_sem):
    part = out.shape[0] // MIX_PARTS
    copies = []
    for c in range(MIX_PARTS):
        at = pl.ds(c * part, part)
        out[at, :] = jnp.dot(
            combine_ref[at, :], slots_ref[...], preferred_element_type=F32
        ).astype(BF16)
        copy = pltpu.make_async_copy(out.at[at, :], out_hbm.at[at, :], out_sem.at[c])
        copy.start()
        copies.append(copy)
    for copy in copies:
        copy.wait()


def body(n, tokens, slot_proj, w_in, w_out):
    count, width = tokens.shape
    slots_all = slot_proj.shape[1]
    slots = slots_all // n
    ff = w_in.shape[2]
    assert w_in.shape[0] == 1 and n & (n - 1) == 0
    hbm_spec = pl.BlockSpec(memory_space=pltpu.HBM)
    vmem_spec = pl.BlockSpec(memory_space=pltpu.VMEM)
    wide = width + STAT
    dma = pltpu.SemaphoreType.DMA
    combine, slot_out = pl.pallas_call(
        functools.partial(route_kernel, n),
        out_shape=[
            jax.ShapeDtypeStruct((count, slots_all), BF16),
            jax.ShapeDtypeStruct((slots_all, width), BF16),
        ],
        in_specs=[hbm_spec] * 4,
        out_specs=[vmem_spec] * 2,
        scratch_shapes=[
            pltpu.VMEM((count, width), BF16),
            pltpu.VMEM((slots_all, width), BF16),
            pltpu.VMEM((width, ff), BF16),
            pltpu.VMEM((ff, width), BF16),
            pltpu.VMEM((slots_all, count), F32),
            pltpu.VMEM((n, slots, wide), BF16),
            pltpu.VMEM((n - 1, slots, wide), BF16),
            pltpu.VMEM((n, slots, width), BF16),
            pltpu.VMEM((slots_all, width), F32),
            dma((TOKEN_PARTS,)),
            dma,
            dma((TOKEN_PARTS,)),
            dma((TOKEN_PARTS,)),
            dma((n - 1,)),
            dma((n - 1,)),
            dma((n - 1,)),
            dma((n - 1,)),
        ],
        compiler_params=pltpu.CompilerParams(
            collective_id=0, has_side_effects=True, vmem_limit_bytes=48 * 1024 * 1024
        ),
        cost_estimate=pl.CostEstimate(
            flops=4 * count * width * slots_all + 4 * slots * width * ff,
            bytes_accessed=2 * (count * width + 2 * width * ff),
            transcendentals=2 * count * slots_all,
        ),
        name="route",
    )(tokens, pltpu.with_memory_space_constraint(slot_proj.T, pltpu.HBM), w_in, w_out)
    return pl.pallas_call(
        mix_kernel,
        out_shape=jax.ShapeDtypeStruct((count, width), BF16),
        in_specs=[vmem_spec] * 2,
        out_specs=hbm_spec,
        scratch_shapes=[pltpu.VMEM((count, width), BF16), dma((MIX_PARTS,))],
        compiler_params=pltpu.CompilerParams(vmem_limit_bytes=32 * 1024 * 1024),
        cost_estimate=pl.CostEstimate(
            flops=2 * count * width * slots_all,
            bytes_accessed=2 * count * width,
            transcendentals=0,
        ),
        name="mix",
    )(combine, slot_out)


def solution(mesh):
    return jax.shard_map(
        functools.partial(body, mesh.shape["seq"]),
        mesh=mesh,
        in_specs=(P(("clip", "seq"), None), P(), P("seq", None, None), P("seq", None, None)),
        out_specs=P(("clip", "seq"), None),
        check_vma=False,
    )
```

```python
import functools

import jax
import jax.numpy as jnp
from jax import lax
from jax.experimental import pallas as pl
from jax.experimental.pallas import tpu as pltpu
from jax.sharding import PartitionSpec as P

MESH = pl.DeviceIdType.MESH
F32 = jnp.float32
BF16 = jnp.bfloat16
TOKEN_PARTS = 5
MIX_PARTS = 20
VECTOR_FF = 768
GROUP = 256
STAT = 128


def split3(x):
    high = x.astype(BF16).astype(F32)
    middle = (x - high).astype(BF16).astype(F32)
    return [high, middle, x - high - middle]


def spread_slots(spread, x):
    slots, depth = x.shape
    columns = jnp.concatenate([x] * (8 // slots), axis=0).T
    for i in range(slots):
        spread[i, :depth, :] = jnp.broadcast_to(columns[:, i : i + 1], (depth, 128)).astype(BF16)


def vector_dot(spread, w, row, depth, column):
    slots = spread.shape[0]
    sums = [jnp.zeros((16, GROUP), F32) for _ in range(slots)]
    for d in range(0, depth, 64):
        tiles = [w[row + d + r : row + d + r + 16, column : column + GROUP] for r in range(0, 64, 16)]
        for i in range(slots):
            terms = []
            for k, tile in enumerate(tiles):
                value = spread[i, d + 16 * k : d + 16 * k + 16, :]
                terms.append(tile * jnp.concatenate([value] * (GROUP // 128), axis=1))
            pair = (terms[0] + terms[1]) + (terms[2] + terms[3])
            sums[i] = sums[i] + pair.astype(F32)
    return jnp.concatenate([jnp.sum(x, axis=0, keepdims=True) for x in sums], axis=0)


def route_kernel(
    n,
    tokens_hbm,
    proj_hbm,
    w_in_hbm,
    w_out_hbm,
    combine_ref,
    slots_ref,
    tok,
    proj,
    w_in,
    w_out,
    logits,
    send,
    recv,
    gather,
    rows,
    spread,
    tok_sem,
    proj_sem,
    in_sem,
    out_sem,
    s1_sem,
    r1_sem,
    s2_sem,
    r2_sem,
):
    me = lax.axis_index("seq")
    width = tok.shape[1]
    slots = send.shape[1]
    part = tok.shape[0] // TOKEN_PARTS
    ff = w_in.shape[1]

    proj_copy = pltpu.make_async_copy(proj_hbm, proj, proj_sem)
    proj_copy.start()
    tok_copies = []
    for c in range(TOKEN_PARTS):
        at = pl.ds(c * part, part)
        copy = pltpu.make_async_copy(tokens_hbm.at[at, :], tok.at[at, :], tok_sem.at[c])
        copy.start()
        tok_copies.append(copy)
    in_copies, out_copies = [], []
    for c in range(TOKEN_PARTS):
        at = pl.ds(c * (width // TOKEN_PARTS), width // TOKEN_PARTS)
        in_copies.append(pltpu.make_async_copy(w_in_hbm.at[0, at, :], w_in.at[at, :], in_sem.at[c]))
        at = pl.ds(c * (ff // TOKEN_PARTS), ff // TOKEN_PARTS)
        out_copies.append(pltpu.make_async_copy(w_out_hbm.at[0, at, :], w_out.at[at, :], out_sem.at[c]))

    barrier = pltpu.get_barrier_semaphore()
    peers = [lax.bitwise_xor(me, n - 1 - k) for k in range(n - 1)]
    for peer in peers:
        pl.semaphore_signal(barrier, inc=1, device_id={"seq": peer}, device_id_type=MESH)

    proj_copy.wait()

    def part_logits(c):
        tok_copies[c].wait()
        in_copies[c].start()
        out_copies[c].start()
        at = slice(c * part, (c + 1) * part)
        l = lax.dot_general(
            proj[...], tok[at, :], (((1,), (1,)), ((), ())), preferred_element_type=F32
        )
        logits[:, at] = l
        return l

    top = total = num = None
    l = part_logits(0)
    for c in range(TOKEN_PARTS):
        if c + 1 < TOKEN_PARTS:
            following = part_logits(c + 1)
        here = jnp.max(l, axis=1, keepdims=True)
        new = here if c == 0 else jnp.maximum(top, here)
        shifted = jnp.exp(l - new)
        t = jnp.sum(shifted, axis=1, keepdims=True)
        x = tok[c * part : (c + 1) * part, :]
        v = jnp.dot(shifted.astype(BF16), x, preferred_element_type=F32)
        if c == 0:
            total, num = t, v
        else:
            keep = jnp.exp(top - new)
            total, num = total * keep + t, num * keep + v
        top, l = new, following

    lane = lax.broadcasted_iota(jnp.int32, (num.shape[0], STAT), 1)
    stats = jnp.zeros((num.shape[0], STAT), F32)
    for i, term in enumerate(split3(top) + split3(total)):
        stats = jnp.where(lane == i, term, stats)
    for e in range(n):
        at = slice(e * slots, (e + 1) * slots)
        send[e, :, :width] = num[at, :].astype(BF16)
        send[e, :, width:] = stats[at, :].astype(BF16)

    pl.semaphore_wait(barrier, n - 1)
    first = []
    for k, peer in enumerate(peers):
        copy = pltpu.make_async_remote_copy(
            src_ref=send.at[peer],
            dst_ref=recv.at[k],
            send_sem=s1_sem.at[k],
            recv_sem=r1_sem.at[k],
            device_id={"seq": peer},
            device_id_type=MESH,
        )
        copy.start()
        first.append(copy)

    l = logits[...]
    e = jnp.exp(l - jnp.max(l, axis=0, keepdims=True))
    combine_ref[...] = (e / jnp.sum(e, axis=0, keepdims=True)).T.astype(BF16)

    for copy in first:
        copy.wait_recv()
    got = [send[me].astype(F32)] + [recv[k].astype(F32) for k in range(n - 1)]
    terms = [[g[:, width + i : width + i + 1] for i in range(6)] for g in got]
    tops = [t[0] + t[1] + t[2] for t in terms]
    top = functools.reduce(jnp.maximum, tops)
    total = jnp.zeros((slots, 1), F32)
    num = jnp.zeros((slots, width), F32)
    for k in range(n):
        scale = jnp.exp(tops[k] - top)
        total = total + scale * (terms[k][3] + terms[k][4] + terms[k][5])
        num = num + scale * got[k][:, :width]
    slot_in = (num / total).astype(BF16)

    for copy in in_copies + out_copies:
        copy.wait()
    split = ff - VECTOR_FF
    spread_slots(spread, slot_in.astype(F32))
    hidden_m, hidden_v = [], []
    for c in range(0, split, GROUP):
        if c < VECTOR_FF:
            hidden_v.append(vector_dot(spread, w_in, 0, width, split + c))
        hidden_m.append(jnp.dot(slot_in, w_in[:, c : c + GROUP], preferred_element_type=F32))
    hidden_v = jax.nn.gelu(jnp.concatenate(hidden_v, axis=1)).astype(BF16)
    hidden_m = jax.nn.gelu(jnp.concatenate(hidden_m, axis=1)).astype(BF16)
    spread_slots(spread, hidden_v.astype(F32))
    slot_out = []
    for c in range(0, width, GROUP):
        v = vector_dot(spread, w_out, split, VECTOR_FF, c)
        m = jnp.dot(hidden_m, w_out[:split, c : c + GROUP], preferred_element_type=F32)
        slot_out.append(m + v)
    slot_out = jnp.concatenate(slot_out, axis=1)
    gather[me] = slot_out.astype(BF16)

    second = []
    for k, peer in enumerate(peers):
        copy = pltpu.make_async_remote_copy(
            src_ref=gather.at[me],
            dst_ref=gather.at[me],
            send_sem=s2_sem.at[k],
            recv_sem=r2_sem.at[k],
            device_id={"seq": peer},
            device_id_type=MESH,
        )
        copy.start()
        second.append(copy)
    for copy in second:
        copy.wait_recv()
    for e in range(n):
        rows[e * slots : (e + 1) * slots, :] = gather[e].astype(F32)
    slots_ref[...] = rows[...].astype(BF16)
    for copy in first + second:
        copy.wait_send()


def mix_kernel(combine_ref, slots_ref, out_hbm, out, out_sem):
    part = out.shape[0] // MIX_PARTS
    copies = []
    for c in range(MIX_PARTS):
        at = pl.ds(c * part, part)
        out[at, :] = jnp.dot(
            combine_ref[at, :], slots_ref[...], preferred_element_type=F32
        ).astype(BF16)
        copy = pltpu.make_async_copy(out.at[at, :], out_hbm.at[at, :], out_sem.at[c])
        copy.start()
        copies.append(copy)
    for copy in copies:
        copy.wait()


def body(n, tokens, slot_proj, w_in, w_out):
    count, width = tokens.shape
    slots_all = slot_proj.shape[1]
    slots = slots_all // n
    ff = w_in.shape[2]
    assert w_in.shape[0] == 1 and n & (n - 1) == 0
    hbm_spec = pl.BlockSpec(memory_space=pltpu.HBM)
    vmem_spec = pl.BlockSpec(memory_space=pltpu.VMEM)
    wide = width + STAT
    dma = pltpu.SemaphoreType.DMA
    combine, slot_out = pl.pallas_call(
        functools.partial(route_kernel, n),
        out_shape=[
            jax.ShapeDtypeStruct((count, slots_all), BF16),
            jax.ShapeDtypeStruct((slots_all, width), BF16),
        ],
        in_specs=[hbm_spec] * 4,
        out_specs=[vmem_spec] * 2,
        scratch_shapes=[
            pltpu.VMEM((count, width), BF16),
            pltpu.VMEM((slots_all, width), BF16),
            pltpu.VMEM((width, ff), BF16),
            pltpu.VMEM((ff, width), BF16),
            pltpu.VMEM((slots_all, count), F32),
            pltpu.VMEM((n, slots, wide), BF16),
            pltpu.VMEM((n - 1, slots, wide), BF16),
            pltpu.VMEM((n, slots, width), BF16),
            pltpu.VMEM((slots_all, width), F32),
            pltpu.VMEM((slots, max(width, VECTOR_FF), 128), BF16),
            dma((TOKEN_PARTS,)),
            dma,
            dma((TOKEN_PARTS,)),
            dma((TOKEN_PARTS,)),
            dma((n - 1,)),
            dma((n - 1,)),
            dma((n - 1,)),
            dma((n - 1,)),
        ],
        compiler_params=pltpu.CompilerParams(
            collective_id=0, has_side_effects=True, vmem_limit_bytes=48 * 1024 * 1024
        ),
        cost_estimate=pl.CostEstimate(
            flops=4 * count * width * slots_all + 4 * slots * width * ff,
            bytes_accessed=2 * (count * width + 2 * width * ff),
            transcendentals=2 * count * slots_all,
        ),
        name="route",
    )(tokens, pltpu.with_memory_space_constraint(slot_proj.T, pltpu.HBM), w_in, w_out)
    return pl.pallas_call(
        mix_kernel,
        out_shape=jax.ShapeDtypeStruct((count, width), BF16),
        in_specs=[vmem_spec] * 2,
        out_specs=hbm_spec,
        scratch_shapes=[pltpu.VMEM((count, width), BF16), dma((MIX_PARTS,))],
        compiler_params=pltpu.CompilerParams(vmem_limit_bytes=32 * 1024 * 1024),
        cost_estimate=pl.CostEstimate(
            flops=2 * count * width * slots_all,
            bytes_accessed=2 * count * width,
            transcendentals=0,
        ),
        name="mix",
    )(combine, slot_out)


def solution(mesh):
    return jax.shard_map(
        functools.partial(body, mesh.shape["seq"]),
        mesh=mesh,
        in_specs=(P(("clip", "seq"), None), P(), P("seq", None, None), P("seq", None, None)),
        out_specs=P(("clip", "seq"), None),
        check_vma=False,
    )
```

```python
import functools

import jax
import jax.numpy as jnp
from jax import lax
from jax.experimental import pallas as pl
from jax.experimental.pallas import tpu as pltpu
from jax.sharding import PartitionSpec as P

MESH = pl.DeviceIdType.MESH
F32 = jnp.float32
BF16 = jnp.bfloat16
TOKEN_CUTS = (0, 1, 3, 5)
TOKEN_PARTS = len(TOKEN_CUTS) - 1
WEIGHT_PARTS = 5
MIX_PARTS = 20
VECTOR_FF = 768
GROUP = 256
STAT = 128


def split3(x):
    high = x.astype(BF16).astype(F32)
    middle = (x - high).astype(BF16).astype(F32)
    return [high, middle, x - high - middle]


def spread_slots(spread, x):
    slots, depth = x.shape
    columns = jnp.concatenate([x] * (8 // slots), axis=0).T
    for i in range(slots):
        spread[i, :depth, :] = jnp.broadcast_to(columns[:, i : i + 1], (depth, 128)).astype(BF16)


def vector_dot(spread, w, row, depth, column):
    slots = spread.shape[0]
    sums = [jnp.zeros((16, GROUP), F32) for _ in range(slots)]
    for d in range(0, depth, 64):
        tiles = [w[row + d + r : row + d + r + 16, column : column + GROUP] for r in range(0, 64, 16)]
        for i in range(slots):
            terms = []
            for k, tile in enumerate(tiles):
                value = spread[i, d + 16 * k : d + 16 * k + 16, :]
                terms.append(tile * jnp.concatenate([value] * (GROUP // 128), axis=1))
            pair = (terms[0] + terms[1]) + (terms[2] + terms[3])
            sums[i] = sums[i] + pair.astype(F32)
    return jnp.concatenate([jnp.sum(x, axis=0, keepdims=True) for x in sums], axis=0)


def route_kernel(
    n,
    tokens_hbm,
    proj_hbm,
    w_in_hbm,
    w_out_hbm,
    combine_ref,
    slots_ref,
    tok,
    proj,
    w_in,
    w_out,
    logits,
    send,
    recv,
    gather,
    rows,
    spread,
    tok_sem,
    proj_sem,
    in_sem,
    out_sem,
    s1_sem,
    r1_sem,
    s2_sem,
    r2_sem,
):
    me = lax.axis_index("seq")
    width = tok.shape[1]
    slots = send.shape[1]
    cuts = [c * (tok.shape[0] // TOKEN_CUTS[-1]) for c in TOKEN_CUTS]
    ff = w_in.shape[1]

    proj_copy = pltpu.make_async_copy(proj_hbm, proj, proj_sem)
    proj_copy.start()
    tok_copies = []
    for c in range(TOKEN_PARTS):
        at = pl.ds(cuts[c], cuts[c + 1] - cuts[c])
        copy = pltpu.make_async_copy(tokens_hbm.at[at, :], tok.at[at, :], tok_sem.at[c])
        copy.start()
        tok_copies.append(copy)
    in_copies, out_copies = [], []
    for c in range(WEIGHT_PARTS):
        at = pl.ds(c * (width // WEIGHT_PARTS), width // WEIGHT_PARTS)
        in_copies.append(pltpu.make_async_copy(w_in_hbm.at[0, at, :], w_in.at[at, :], in_sem.at[c]))
        at = pl.ds(c * (ff // WEIGHT_PARTS), ff // WEIGHT_PARTS)
        out_copies.append(pltpu.make_async_copy(w_out_hbm.at[0, at, :], w_out.at[at, :], out_sem.at[c]))

    barrier = pltpu.get_barrier_semaphore()
    peers = [lax.bitwise_xor(me, n - 1 - k) for k in range(n - 1)]
    for peer in peers:
        pl.semaphore_signal(barrier, inc=1, device_id={"seq": peer}, device_id_type=MESH)

    proj_copy.wait()

    def part_logits(c):
        tok_copies[c].wait()
        begun = slice(TOKEN_CUTS[c], TOKEN_CUTS[c + 1])
        for copy in in_copies[begun] + out_copies[begun]:
            copy.start()
        at = slice(cuts[c], cuts[c + 1])
        l = lax.dot_general(
            proj[...], tok[at, :], (((1,), (1,)), ((), ())), preferred_element_type=F32
        )
        logits[:, at] = l
        return l

    top = total = num = None
    l = part_logits(0)
    for c in range(TOKEN_PARTS):
        if c + 1 < TOKEN_PARTS:
            following = part_logits(c + 1)
        here = jnp.max(l, axis=1, keepdims=True)
        new = here if c == 0 else jnp.maximum(top, here)
        shifted = jnp.exp(l - new)
        t = jnp.sum(shifted, axis=1, keepdims=True)
        x = tok[cuts[c] : cuts[c + 1], :]
        v = jnp.dot(shifted.astype(BF16), x, preferred_element_type=F32)
        if c == 0:
            total, num = t, v
        else:
            keep = jnp.exp(top - new)
            total, num = total * keep + t, num * keep + v
        top, l = new, following

    lane = lax.broadcasted_iota(jnp.int32, (num.shape[0], STAT), 1)
    stats = jnp.zeros((num.shape[0], STAT), F32)
    for i, term in enumerate(split3(top) + split3(total)):
        stats = jnp.where(lane == i, term, stats)
    for e in range(n):
        at = slice(e * slots, (e + 1) * slots)
        send[e, :, :width] = num[at, :].astype(BF16)
        send[e, :, width:] = stats[at, :].astype(BF16)

    pl.semaphore_wait(barrier, n - 1)
    first = []
    for k, peer in enumerate(peers):
        copy = pltpu.make_async_remote_copy(
            src_ref=send.at[peer],
            dst_ref=recv.at[k],
            send_sem=s1_sem.at[k],
            recv_sem=r1_sem.at[k],
            device_id={"seq": peer},
            device_id_type=MESH,
        )
        copy.start()
        first.append(copy)

    l = logits[...]
    e = jnp.exp(l - jnp.max(l, axis=0, keepdims=True))
    combine_ref[...] = (e / jnp.sum(e, axis=0, keepdims=True)).T.astype(BF16)

    for copy in first:
        copy.wait_recv()
    got = [send[me].astype(F32)] + [recv[k].astype(F32) for k in range(n - 1)]
    terms = [[g[:, width + i : width + i + 1] for i in range(6)] for g in got]
    tops = [t[0] + t[1] + t[2] for t in terms]
    top = functools.reduce(jnp.maximum, tops)
    total = jnp.zeros((slots, 1), F32)
    num = jnp.zeros((slots, width), F32)
    for k in range(n):
        scale = jnp.exp(tops[k] - top)
        total = total + scale * (terms[k][3] + terms[k][4] + terms[k][5])
        num = num + scale * got[k][:, :width]
    slot_in = (num / total).astype(BF16)

    for copy in in_copies + out_copies:
        copy.wait()
    split = ff - VECTOR_FF
    spread_slots(spread, slot_in.astype(F32))
    hidden_m, hidden_v = [], []
    for c in range(0, split, GROUP):
        if c < VECTOR_FF:
            hidden_v.append(vector_dot(spread, w_in, 0, width, split + c))
        hidden_m.append(jnp.dot(slot_in, w_in[:, c : c + GROUP], preferred_element_type=F32))
    hidden_v = jax.nn.gelu(jnp.concatenate(hidden_v, axis=1)).astype(BF16)
    hidden_m = jax.nn.gelu(jnp.concatenate(hidden_m, axis=1)).astype(BF16)
    spread_slots(spread, hidden_v.astype(F32))
    slot_out = []
    for c in range(0, width, GROUP):
        v = vector_dot(spread, w_out, split, VECTOR_FF, c)
        m = jnp.dot(hidden_m, w_out[:split, c : c + GROUP], preferred_element_type=F32)
        slot_out.append(m + v)
    slot_out = jnp.concatenate(slot_out, axis=1)
    gather[me] = slot_out.astype(BF16)

    second = []
    for k, peer in enumerate(peers):
        copy = pltpu.make_async_remote_copy(
            src_ref=gather.at[me],
            dst_ref=gather.at[me],
            send_sem=s2_sem.at[k],
            recv_sem=r2_sem.at[k],
            device_id={"seq": peer},
            device_id_type=MESH,
        )
        copy.start()
        second.append(copy)
    for copy in second:
        copy.wait_recv()
    for e in range(n):
        rows[e * slots : (e + 1) * slots, :] = gather[e].astype(F32)
    slots_ref[...] = rows[...].astype(BF16)
    for copy in first + second:
        copy.wait_send()


def mix_kernel(combine_ref, slots_ref, out_hbm, out, out_sem):
    part = out.shape[0] // MIX_PARTS
    copies = []
    for c in range(MIX_PARTS):
        at = pl.ds(c * part, part)
        out[at, :] = jnp.dot(
            combine_ref[at, :], slots_ref[...], preferred_element_type=F32
        ).astype(BF16)
        copy = pltpu.make_async_copy(out.at[at, :], out_hbm.at[at, :], out_sem.at[c])
        copy.start()
        copies.append(copy)
    for copy in copies:
        copy.wait()


def body(n, tokens, slot_proj, w_in, w_out):
    count, width = tokens.shape
    slots_all = slot_proj.shape[1]
    slots = slots_all // n
    ff = w_in.shape[2]
    assert w_in.shape[0] == 1 and n & (n - 1) == 0
    hbm_spec = pl.BlockSpec(memory_space=pltpu.HBM)
    vmem_spec = pl.BlockSpec(memory_space=pltpu.VMEM)
    wide = width + STAT
    dma = pltpu.SemaphoreType.DMA
    combine, slot_out = pl.pallas_call(
        functools.partial(route_kernel, n),
        out_shape=[
            jax.ShapeDtypeStruct((count, slots_all), BF16),
            jax.ShapeDtypeStruct((slots_all, width), BF16),
        ],
        in_specs=[hbm_spec] * 4,
        out_specs=[vmem_spec] * 2,
        scratch_shapes=[
            pltpu.VMEM((count, width), BF16),
            pltpu.VMEM((slots_all, width), BF16),
            pltpu.VMEM((width, ff), BF16),
            pltpu.VMEM((ff, width), BF16),
            pltpu.VMEM((slots_all, count), F32),
            pltpu.VMEM((n, slots, wide), BF16),
            pltpu.VMEM((n - 1, slots, wide), BF16),
            pltpu.VMEM((n, slots, width), BF16),
            pltpu.VMEM((slots_all, width), F32),
            pltpu.VMEM((slots, max(width, VECTOR_FF), 128), BF16),
            dma((TOKEN_PARTS,)),
            dma,
            dma((WEIGHT_PARTS,)),
            dma((WEIGHT_PARTS,)),
            dma((n - 1,)),
            dma((n - 1,)),
            dma((n - 1,)),
            dma((n - 1,)),
        ],
        compiler_params=pltpu.CompilerParams(
            collective_id=0, has_side_effects=True, vmem_limit_bytes=48 * 1024 * 1024
        ),
        cost_estimate=pl.CostEstimate(
            flops=4 * count * width * slots_all + 4 * slots * width * ff,
            bytes_accessed=2 * (count * width + 2 * width * ff),
            transcendentals=2 * count * slots_all,
        ),
        name="route",
    )(tokens, pltpu.with_memory_space_constraint(slot_proj.T, pltpu.HBM), w_in, w_out)
    return pl.pallas_call(
        mix_kernel,
        out_shape=jax.ShapeDtypeStruct((count, width), BF16),
        in_specs=[vmem_spec] * 2,
        out_specs=hbm_spec,
        scratch_shapes=[pltpu.VMEM((count, width), BF16), dma((MIX_PARTS,))],
        compiler_params=pltpu.CompilerParams(vmem_limit_bytes=32 * 1024 * 1024),
        cost_estimate=pl.CostEstimate(
            flops=2 * count * width * slots_all,
            bytes_accessed=2 * count * width,
            transcendentals=0,
        ),
        name="mix",
    )(combine, slot_out)


def solution(mesh):
    return jax.shard_map(
        functools.partial(body, mesh.shape["seq"]),
        mesh=mesh,
        in_specs=(P(("clip", "seq"), None), P(), P("seq", None, None), P("seq", None, None)),
        out_specs=P(("clip", "seq"), None),
        check_vma=False,
    )
```
